32 devices in a mesh: seq: 4 (over x, core), blk: 8 (over z, y).
Axes of the slice: x: 2, y: 2, z: 4, core: 2. Of those that a mesh axis runs over, the one named last changes fastest.
Arguments:
- patches: bfloat16 [8192, 1280], P(('seq', 'blk')), may hold values from -40 to 40
- vis_gain: float32 [1280], replicated, may hold values from 0.1 to 1.9
- vis_up: bfloat16 [5120, 1280], P('seq'), may hold values from -0.15625 to 0.15625
- vis_bias: float32 [5120], P('seq'), may hold values from -4 to 4
- vis_down: bfloat16 [5120, 1280], P('seq'), may hold values from -0.078125 to 0.078125
- merge_gain: float32 [1280], replicated, may hold values from 0.1 to 1.9
- merge_proj: bfloat16 [5120, 1280], replicated, may hold values from -0.078125 to 0.078125
- text_embed: bfloat16 [4096, 1280], P(('seq', 'blk')), may hold values from -40 to 40
- slot_index: int32 [2048], P(('seq', 'blk')), may hold values from 0 to 4095, as said below
- text_gain: float32 [1280], replicated, may hold values from 0.1 to 1.9
- text_up: bfloat16 [5120, 1280], P('blk'), may hold values from -0.15625 to 0.15625
- text_down: bfloat16 [5120, 1280], P('blk'), may hold values from -0.078125 to 0.078125
Outputs:
- hidden_out: bfloat16 [4096, 1280], P(('seq', 'blk'))
The draws below stay inside these ranges and needn't reach their ends.
Inputs may be any that keep to these rules, and one draw needn't show every extreme that they name: slot_index values are distinct. The merged rows held by one device go to prompt tokens held by devices with the same seq index. Each device sends either no merged rows or exactly 16 merged rows to each device of its blk group; in every draw some device receives 16 rows from every device of its blk group.
All inputs are finite; a program needn't handle non-finite values.
Results may differ from the reference program's by a relative error of at most 0.015.
Values may be sent and summed in bfloat16 or wider, within the bound.
No kernel may reach another device: no remote copies, remote signals or barrier semaphores. Data moves between devices by JAX's collectives and lax.ppermute only.
A program may use at most 192 MiB of HBM per device.

```python
import math
import jax
import jax.numpy as jnp
from jax import lax

D = 1280
FF = 5120
TFF = 5120
MD = 5120
P_DEV = 256
T_DEV = 128
M_DEV = 64
CAP = 16
PATCHES = 8192
MERGED = 2048
TOKENS = 4096


def scaled_rows(key, row_total, col_total):
    key_base, key_rows, key_cols = jax.random.split(key, 3)
    base = jnp.clip(jax.random.normal(key_base, (row_total, col_total), jnp.float32), -4.0, 4.0)
    row_scale = jnp.exp(jax.random.uniform(key_rows, (row_total, 1), jnp.float32, math.log(0.3), math.log(3.0)))
    col_scale = jnp.exp(jax.random.uniform(key_cols, (1, col_total), jnp.float32, math.log(0.3), math.log(3.0)))
    return (base * row_scale * col_scale).astype(jnp.bfloat16)


def draw_patches(key, part):
    return scaled_rows(jax.random.fold_in(key, 11), PATCHES, D)


def draw_text_embed(key, part):
    return scaled_rows(jax.random.fold_in(key, 12), TOKENS, D)


def draw_slot_index(key, part):
    cycle_size = 2 * M_DEV // CAP
    window = cycle_size // 2
    group_total = TOKENS // (T_DEV * cycle_size)

    def one_group(group_key, group_number):
        key_base, key_start, key_perm = jax.random.split(group_key, 3)
        centre = jax.random.randint(key_base, (), 0, cycle_size)
        starts = (centre - jax.random.randint(key_start, (cycle_size,), 0, window)) % cycle_size
        steps_in = jnp.arange(window, dtype=jnp.int32)
        targets = (starts[:, None] + steps_in[None, :]) % cycle_size
        devices = jnp.arange(cycle_size, dtype=jnp.int32)
        covers = ((devices[None, :] - starts[:, None]) % cycle_size < window).astype(jnp.int32)
        before = jnp.cumsum(covers, axis=0) - covers
        orders = jax.vmap(lambda perm_key: jax.random.permutation(perm_key, T_DEV).astype(jnp.int32))(jax.random.split(key_perm, cycle_size))
        sources = jnp.arange(cycle_size, dtype=jnp.int32)[:, None, None]
        within = jnp.arange(CAP, dtype=jnp.int32)[None, None, :]
        target_full = targets[:, :, None]
        ranks = CAP * before[sources, target_full] + within
        position = orders[target_full, ranks]
        slots = group_number * cycle_size * T_DEV + target_full * T_DEV + position
        return slots.reshape(cycle_size * M_DEV).astype(jnp.int32)
    keys_all = jax.random.split(jax.random.fold_in(key, 13), group_total)
    numbers = jnp.arange(group_total, dtype=jnp.int32)
    return jax.vmap(one_group)(keys_all, numbers).reshape(MERGED).astype(jnp.int32)


def block_levels(stream_key, shape, pieces, least, high):
    factor_of, own = 1.0, jax.random.fold_in(stream_key, 6)
    for dim, blocks in pieces:
        heights = jnp.exp(jax.random.uniform(jax.random.fold_in(own, dim), (blocks,), jnp.float32, least / len(pieces), high / len(pieces)))
        factor_of = factor_of * jnp.repeat(heights, shape[dim] // blocks).reshape([-1 if axis == dim else 1 for axis in range(len(shape))])
    return factor_of


def bell_draw(stream_key, dims, scale, limit, cuts=(), held_as=jnp.bfloat16):
    factor_of = block_levels(stream_key, dims, cuts, -0.22, 0.18) if cuts else 1.0
    result = jax.random.normal(stream_key, dims, jnp.float32) * scale * factor_of
    return jnp.minimum(jnp.maximum(result, -limit), limit).astype(held_as)


def setup_inputs(seed: int = 0) -> dict:
    keys = jax.random.split(jax.random.key(seed), 13)
    return {
        "patches": draw_patches(jax.random.fold_in(keys[12], 71), 0),
        "vis_gain": jnp.clip(1.0 + 0.18 * jax.random.normal(keys[1], (D,), jnp.float32), 0.1, 1.9),
        "vis_up": bell_draw(keys[2], (FF, D), D ** -0.5, 0.15625, ((0, 4),)),
        "vis_bias": bell_draw(keys[3], (FF,), 1.0, 4.0, ((0, 4),), jnp.float32),
        "vis_down": bell_draw(keys[4], (FF, D), FF ** -0.5, 0.078125, ((0, 4),)),
        "merge_gain": jnp.clip(1.0 + 0.18 * jax.random.normal(keys[5], (D,), jnp.float32), 0.1, 1.9),
        "merge_proj": bell_draw(keys[6], (MD, D), MD ** -0.5, 0.078125),
        "text_embed": draw_text_embed(jax.random.fold_in(keys[12], 71), 0),
        "slot_index": draw_slot_index(jax.random.fold_in(keys[12], 71), 0),
        "text_gain": jnp.clip(1.0 + 0.18 * jax.random.normal(keys[9], (D,), jnp.float32), 0.1, 1.9),
        "text_up": bell_draw(keys[10], (TFF, D), D ** -0.5, 0.15625, ((0, 8),)),
        "text_down": bell_draw(keys[11], (TFF, D), TFF ** -0.5, 0.078125, ((0, 8),)),
    }


def normalize(values, row_gain):
    values = values.astype(jnp.float32)
    center = values - lax.optimization_barrier(jnp.mean(values, axis=-1, keepdims=True))
    spread = lax.optimization_barrier(jnp.mean(center * center, axis=-1, keepdims=True))
    return center * lax.rsqrt(spread + 1e-06) * row_gain

def vision_block(rows_in, vis_gain, vis_up, vis_bias, vis_down, merge_gain, merge_proj):
    normed = normalize(rows_in, vis_gain).astype(jnp.bfloat16)
    pre_act = jnp.dot(normed, vis_up.T, preferred_element_type=jnp.float32) + vis_bias
    hidden = jax.nn.gelu(pre_act, approximate=True).astype(jnp.bfloat16)
    vis_out = rows_in.astype(jnp.float32) + jnp.dot(hidden, vis_down, preferred_element_type=jnp.float32)
    merge_normed = normalize(vis_out, merge_gain).astype(jnp.bfloat16)
    joined = merge_normed.reshape(merge_normed.shape[0] // 4, 4 * merge_normed.shape[1])
    return jnp.dot(joined, merge_proj, preferred_element_type=jnp.float32).astype(jnp.bfloat16)

def text_block(rows_in, text_gain, text_up, text_down):
    normed = normalize(rows_in, text_gain).astype(jnp.bfloat16)
    hidden = jax.nn.gelu(jnp.dot(normed, text_up.T, preferred_element_type=jnp.float32), approximate=True).astype(jnp.bfloat16)
    summed = rows_in.astype(jnp.float32) + jnp.dot(hidden, text_down, preferred_element_type=jnp.float32)
    return summed.astype(jnp.bfloat16)

def reference(patches, vis_gain, vis_up, vis_bias, vis_down, merge_gain, merge_proj, text_embed, slot_index, text_gain, text_up, text_down):
    stacked = patches.reshape(PATCHES // P_DEV, P_DEV, D)
    merged = lax.map(lambda rows_in: vision_block(rows_in, vis_gain, vis_up, vis_bias, vis_down, merge_gain, merge_proj), stacked)
    merged = merged.reshape(MERGED, D)
    text_rows = text_embed.at[slot_index].set(merged)
    outputs = lax.map(lambda rows_in: text_block(rows_in, text_gain, text_up, text_down), text_rows.reshape(TOKENS // T_DEV, T_DEV, D))
    return outputs.reshape(TOKENS, D)
```

```python
import functools

import jax
import jax.numpy as jnp
from jax import lax
from jax.experimental import pallas as pl
from jax.experimental.pallas import tpu as pltpu
from jax.sharding import PartitionSpec as P

F32 = jnp.float32
BF16 = jnp.bfloat16
ANY = pl.BlockSpec(memory_space=pl.ANY)
VMEM = pl.BlockSpec(memory_space=pltpu.VMEM)
PARAMS = pltpu.CompilerParams(vmem_limit_bytes=48 * 1024 * 1024)


def normalize(values, row_gain):
    values = values.astype(F32)
    center = values - jnp.mean(values, axis=-1, keepdims=True)
    spread = jnp.mean(center * center, axis=-1, keepdims=True)
    return center * lax.rsqrt(spread + 1e-06) * row_gain


def gelu(v):
    return 0.5 * v * (1.0 + jnp.tanh(0.7978845608028654 * (v + 0.044715 * (v * v * v))))


def up_project(rows_in, up_piece):
    return lax.dot_general(rows_in, up_piece, (((1,), (1,)), ((), ())), preferred_element_type=F32)


def swap(x, axis, bit):
    size = lax.axis_size(axis)
    return lax.ppermute(x, axis, [(i, i ^ bit) for i in range(size)])


def plane_rows(patches):
    rows = patches.shape[0]
    count = rows // 8
    place = lax.broadcasted_iota(jnp.int32, (rows, rows), 0)
    source = lax.broadcasted_iota(jnp.int32, (rows, rows), 1)
    half, plane, window = place // (4 * count), place // count % 4, place % count
    order = (source == 4 * (count * half + window) + plane).astype(BF16)
    return jnp.dot(order, patches, preferred_element_type=F32)


def norm_patches_kernel(patches_ref, gain_ref, first_ref, second_ref):
    rows = patches_ref.shape[0]
    normed = normalize(plane_rows(patches_ref[...]), gain_ref[...]).astype(BF16)
    first_ref[...] = normed[: rows // 2]
    second_ref[...] = normed[rows // 2 :]


def norm_patches(patches, gain):
    rows, width = patches.shape
    half = jax.ShapeDtypeStruct((rows // 2, width), BF16)
    return pl.pallas_call(
        norm_patches_kernel,
        out_shape=(half, half),
        in_specs=[VMEM, VMEM],
        out_specs=(VMEM, VMEM),
        compiler_params=PARAMS,
        name="norm_patches",
    )(patches, gain.reshape(1, width))


def load_tiles(tiles, scratch, sems):
    copies, number = [], 0
    for place, pieces in enumerate(tiles):
        at, mine = 0, []
        for ref, first, rows in pieces:
            copy = pltpu.make_async_copy(
                ref.at[pl.ds(first, rows)], scratch.at[place, pl.ds(at, rows)], sems.at[number]
            )
            copy.start()
            mine.append(copy)
            at += rows
            number += 1
        copies.append(mine)
    return copies


def feed_forward(rows, biases, up_copies, up, down_copies, down):
    total = None
    for tile in range(len(up_copies)):
        for copy in up_copies[tile]:
            copy.wait()
        hidden = up_project(rows, up[tile])
        if biases is not None:
            hidden = hidden + biases[tile]
        hidden = gelu(hidden).astype(BF16)
        for copy in down_copies[tile]:
            copy.wait()
        part = jnp.dot(hidden, down[tile], preferred_element_type=F32)
        total = part if total is None else total + part
    return total


def vision_kernel(row_count, *refs):
    row_refs = refs[:row_count]
    up_a, bias_a, down_a, up_b, bias_b, down_b, out_ref, up, down, up_sems, down_sems = refs[row_count:]
    tile = up.shape[1]
    spans = range(0, up_a.shape[0], tile)
    up_copies = load_tiles([[(ref, at, tile)] for ref in (up_a, up_b) for at in spans], up, up_sems)
    down_copies = load_tiles([[(ref, at, tile)] for ref in (down_a, down_b) for at in spans], down, down_sems)
    biases = [ref[:, pl.ds(at, tile)] for ref in (bias_a, bias_b) for at in spans]
    rows = jnp.concatenate([ref[...] for ref in row_refs], axis=0) if row_count > 1 else row_refs[0][...]
    total = feed_forward(rows, biases, up_copies, up, down_copies, down)
    out_ref[...] = total.astype(out_ref.dtype)


def vision_feed_forward(row_parts, weights, out_type):
    (up_a, bias_a, down_a), (up_b, bias_b, down_b) = weights
    width = up_a.shape[1]
    units = up_a.shape[0]
    tile = units // 2
    tiles = 4
    rows = sum(part.shape[0] for part in row_parts)
    return pl.pallas_call(
        functools.partial(vision_kernel, len(row_parts)),
        out_shape=jax.ShapeDtypeStruct((rows, width), out_type),
        in_specs=[VMEM] * len(row_parts) + [ANY, VMEM, ANY, ANY, VMEM, ANY],
        out_specs=VMEM,
        scratch_shapes=[
            pltpu.VMEM((tiles, tile, width), BF16),
            pltpu.VMEM((tiles, tile, width), BF16),
            pltpu.SemaphoreType.DMA((tiles,)),
            pltpu.SemaphoreType.DMA((tiles,)),
        ],
        compiler_params=PARAMS,
        cost_estimate=pl.CostEstimate(
            flops=8 * rows * width * units, bytes_accessed=8 * width * units, transcendentals=2 * rows * units
        ),
        name="vision_feed_forward",
    )(*row_parts, up_a, bias_a.reshape(1, units), down_a, up_b, bias_b.reshape(1, units), down_b)


def merge_kernel(patches_ref, own_ref, first_ref, second_ref, gain_ref, proj_ref, place_ref, out_ref, proj, sems):
    rows, width = patches_ref.shape
    count = rows // 8
    copies = load_tiles([[(proj_ref, plane * width, width)] for plane in range(4)], proj, sems)
    wide = plane_rows(patches_ref[...])
    merged = None
    for plane in range(4):
        halves = []
        for half, back_ref in enumerate((first_ref, second_ref)):
            vis_out = (
                wide[4 * count * half + plane * count :][:count]
                + own_ref[pl.ds(4 * count * half + plane * count, count), :]
                + back_ref[pl.ds(plane * count, count), :].astype(F32)
            )
            halves.append(normalize(vis_out, gain_ref[...]).astype(BF16))
        copies[plane][0].wait()
        part = jnp.dot(jnp.concatenate(halves, axis=0), proj[plane], preferred_element_type=F32)
        merged = part if merged is None else merged + part
    placed = jnp.dot(place_ref[...], merged.astype(BF16), preferred_element_type=F32)
    out_ref[...] = placed.astype(BF16)


def merge_rows(patches, own, first, second, gain, proj, place):
    rows, width = patches.shape
    return pl.pallas_call(
        merge_kernel,
        out_shape=jax.ShapeDtypeStruct((place.shape[0], width), BF16),
        in_specs=[VMEM] * 5 + [ANY, VMEM],
        out_specs=VMEM,
        scratch_shapes=[
            pltpu.VMEM((4, width, width), BF16),
            pltpu.SemaphoreType.DMA((4,)),
        ],
        compiler_params=PARAMS,
        cost_estimate=pl.CostEstimate(
            flops=2 * rows * width * width, bytes_accessed=8 * width * width, transcendentals=rows
        ),
        name="merge_rows",
    )(patches, own, first, second, gain.reshape(1, width), proj, place)


def text_kernel(piece_count, embed_ref, got_ref, pick_ref, gain_ref, up_ref, down_ref, *refs):
    pieces = refs[:piece_count]
    out_ref, up, down, up_sems, down_sems = refs[piece_count:]
    units = up_ref.shape[0]
    part = pieces[0].shape[0] // 2
    per_tile = units // part
    groups = [pieces[at : at + per_tile] for at in range(0, piece_count, per_tile)]
    up_copies = load_tiles(
        [[(up_ref, 0, units)]] + [[(ref, 0, part) for ref in group] for group in groups], up, up_sems
    )
    down_copies = load_tiles(
        [[(down_ref, 0, units)]] + [[(ref, part, part) for ref in group] for group in groups], down, down_sems
    )
    pick = pick_ref[...]
    picked = jnp.dot(pick, got_ref[...], preferred_element_type=F32)
    taken = jnp.sum(pick.astype(F32), axis=1, keepdims=True)
    text_rows = jnp.where(taken > 0.5, picked, embed_ref[...].astype(F32))
    normed = normalize(text_rows, gain_ref[...]).astype(BF16)
    total = feed_forward(normed, None, up_copies, up, down_copies, down)
    if out_ref.dtype == F32:
        total = text_rows + total
    out_ref[...] = total.astype(out_ref.dtype)


def text_feed_forward(embed, got, pick, gain, up, down, pieces, out_type):
    rows, width = embed.shape
    units = up.shape[0]
    loads = 1 + len(pieces)
    tiles = 4
    return pl.pallas_call(
        functools.partial(text_kernel, len(pieces)),
        out_shape=jax.ShapeDtypeStruct((rows, width), out_type),
        in_specs=[VMEM] * 4 + [ANY] * (2 + len(pieces)),
        out_specs=VMEM,
        scratch_shapes=[
            pltpu.VMEM((tiles, units, width), BF16),
            pltpu.VMEM((tiles, units, width), BF16),
            pltpu.SemaphoreType.DMA((loads,)),
            pltpu.SemaphoreType.DMA((loads,)),
        ],
        compiler_params=PARAMS,
        cost_estimate=pl.CostEstimate(
            flops=16 * rows * width * units, bytes_accessed=16 * width * units, transcendentals=4 * rows * units
        ),
        name="text_feed_forward",
    )(embed, got, pick, gain.reshape(1, width), up, down, *pieces)


def gather_text_weights(text_up, text_down):
    units = text_up.shape[0]
    core = lax.axis_index("seq") % 2
    quarter = units // 4
    halves = []
    for half in range(2):
        first = core * (units // 2) + half * quarter
        halves.append(
            jnp.concatenate(
                [lax.dynamic_slice_in_dim(w, first, quarter, 0) for w in (text_up, text_down)], axis=0
            )
        )
    near_a, near_b = swap(halves[0], "blk", 1), swap(halves[1], "blk", 1)
    far_a, far_b = swap(halves[0], "blk", 2), swap(halves[1], "blk", 2)
    both_a, both_b = swap(far_a, "blk", 1), swap(near_b, "blk", 2)
    arrived = [(near_a, near_b), (far_a, far_b), (both_a, both_b)]
    pieces = []
    for pair in arrived:
        pieces += [*pair, *(swap(w, "seq", 1) for w in pair)]
    return pieces


def vision_part(patches, vis_gain, vis_up, vis_bias, vis_down):
    weights = [(vis_up, vis_bias, vis_down), tuple(swap(w, "seq", 1) for w in (vis_up, vis_bias, vis_down))]
    first, second = norm_patches(patches, vis_gain)
    far_first, far_second = swap(first, "seq", 2), swap(second, "seq", 2)
    back_first = swap(vision_feed_forward([far_first], weights, BF16), "seq", 2)
    back_second = swap(vision_feed_forward([far_second], weights, BF16), "seq", 2)
    own = vision_feed_forward([first, second], weights, F32)
    return own, back_first, back_second


def rank_of(target, cycle_size):
    one_hot = (target[..., None] == jnp.arange(cycle_size, dtype=jnp.int32)).astype(jnp.int32)
    return jnp.sum((jnp.cumsum(one_hot, axis=-2) - one_hot) * one_hot, axis=-1)


def per_device(
    patches,
    vis_gain,
    vis_up,
    vis_bias,
    vis_down,
    merge_gain,
    merge_proj,
    text_embed,
    slot_index,
    text_gain,
    text_up,
    text_down,
):
    cycle_size = lax.axis_size("blk")
    merged_count = slot_index.shape[0]
    token_count, width = text_embed.shape
    capacity = 2 * merged_count // cycle_size
    me = lax.axis_index("blk")
    paired = cycle_size == 8

    slots = lax.all_gather(slot_index, "blk", axis=0)
    target = slots // token_count % cycle_size
    position = slots % token_count
    rank = rank_of(target, cycle_size)
    my_target = lax.dynamic_index_in_dim(target, me, 0, keepdims=False)
    my_rank = lax.dynamic_index_in_dim(rank, me, 0, keepdims=False)
    sides = 2 if paired else 1
    dest = jnp.arange(cycle_size, dtype=jnp.int32)[:, None, None, None]
    side = jnp.arange(sides, dtype=jnp.int32)[None, :, None, None]
    nth = jnp.arange(capacity, dtype=jnp.int32)[None, None, :, None]
    owner = dest ^ (4 * side)
    place = ((my_target == owner) & (my_rank == nth)).astype(BF16)
    place = place.reshape(cycle_size * sides * capacity, merged_count)

    def pick_for(which):
        theirs = (target == (me ^ (4 * which)))[:, None, :] & (
            rank[:, None, :] == jnp.arange(capacity, dtype=jnp.int32)[None, :, None]
        )
        where = jnp.max(jnp.where(theirs, position[:, None, :], -1), axis=-1)
        tokens = jnp.arange(token_count, dtype=jnp.int32)[:, None, None]
        chosen = (where[None] == tokens).astype(BF16)
        blank = jnp.zeros_like(chosen)
        parts = [chosen if s == which else blank for s in range(sides)]
        return jnp.stack(parts, axis=2).reshape(token_count, cycle_size * sides * capacity)

    if paired:
        pieces = gather_text_weights(text_up, text_down)
        other_embed = swap(text_embed, "blk", 4)
    own, back_first, back_second = vision_part(patches, vis_gain, vis_up, vis_bias, vis_down)
    send = merge_rows(patches, own, back_first, back_second, merge_gain, merge_proj, place)
    got = lax.all_to_all(send, "blk", split_axis=0, concat_axis=0, tiled=True)
    if paired:
        theirs = text_feed_forward(
            other_embed, got, pick_for(1), text_gain, text_up, text_down, pieces, BF16
        )
        mine = text_feed_forward(text_embed, got, pick_for(0), text_gain, text_up, text_down, pieces, F32)
        return (mine + swap(theirs, "blk", 4).astype(F32)).astype(BF16)
    pick = pick_for(0)
    taken = jnp.sum(pick.astype(F32), axis=1, keepdims=True) > 0.5
    text_rows = jnp.where(taken, jnp.dot(pick, got, preferred_element_type=F32), text_embed.astype(F32))
    text_normed = normalize(text_rows, text_gain).astype(BF16)
    gathered_tokens = lax.all_gather(text_normed, "blk", axis=0, tiled=True)
    hidden = gelu(up_project(gathered_tokens, text_up)).astype(BF16)
    text_mlp = lax.psum_scatter(
        jnp.dot(hidden, text_down, preferred_element_type=F32).astype(BF16),
        "blk",
        scatter_dimension=0,
        tiled=True,
    ).astype(F32)
    return (text_rows + text_mlp).astype(BF16)


def solution(mesh):
    placed = (
        P(("seq", "blk"), None),
        P(),
        P("seq", None),
        P("seq"),
        P("seq", None),
        P(),
        P(),
        P(("seq", "blk"), None),
        P(("seq", "blk")),
        P(),
        P("blk", None),
        P("blk", None),
    )
    return jax.shard_map(
        per_device, mesh=mesh, in_specs=placed, out_specs=P(("seq", "blk"), None), check_vma=False
    )
```

```python
import functools

import jax
import jax.numpy as jnp
from jax import lax
from jax.experimental import pallas as pl
from jax.experimental.pallas import tpu as pltpu
from jax.sharding import PartitionSpec as P

F32 = jnp.float32
BF16 = jnp.bfloat16
VMEM = pl.BlockSpec(memory_space=pltpu.VMEM)
STORED = pl.BlockSpec(memory_space=pltpu.HBM)
SMEM = pl.BlockSpec(memory_space=pltpu.SMEM)
TOKEN = jax.ShapeDtypeStruct((8, 128), F32)


def like(x):
    return jax.ShapeDtypeStruct(x.shape, x.dtype)


def cost(microseconds):
    return pl.CostEstimate(flops=int(microseconds * 1e9), bytes_accessed=1000, transcendentals=0)


def call(kernel, name, out_shape, args, microseconds=0.001, aliases=None, scalars=0, stored=(), copies=0, scratch=(), megabytes=16):
    aliases = aliases or {}
    stored = (*stored, *aliases)
    specs = [SMEM] * scalars + [STORED if at in stored else VMEM for at in range(scalars, len(args))]
    single = not isinstance(out_shape, tuple)
    out_shape = (out_shape,) if single else out_shape
    outs = pl.pallas_call(
        kernel,
        out_shape=out_shape,
        in_specs=specs,
        out_specs=tuple(STORED if at in aliases.values() else VMEM for at in range(len(out_shape))),
        input_output_aliases=aliases,
        scratch_shapes=[*scratch, *([pltpu.SemaphoreType.DMA((copies,))] if copies else [])],
        compiler_params=pltpu.CompilerParams(vmem_limit_bytes=megabytes * 1024 * 1024),
        cost_estimate=cost(microseconds),
        name=name,
    )(*args)
    return outs[0] if single else outs


def normalize(values, row_gain):
    values = values.astype(F32)
    center = values - jnp.mean(values, axis=-1, keepdims=True)
    spread = jnp.mean(center * center, axis=-1, keepdims=True)
    return center * lax.rsqrt(spread + 1e-06) * row_gain


def gelu(v):
    half = 0.5 * v
    return half + half * jnp.tanh(v * (0.7978845608028654 + 0.035677408136300125 * (v * v)))


def up_project(rows_in, up_piece):
    return lax.dot_general(rows_in, up_piece, (((1,), (1,)), ((), ())), preferred_element_type=F32)


def swap(x, axis, bit):
    size = lax.axis_size(axis)
    return lax.ppermute(x, axis, [(i, i ^ bit) for i in range(size)])


def swap_by_core(x, bit_of_core):
    seq_size, blk_size = lax.axis_size("seq"), lax.axis_size("blk")
    pairs = [(s * blk_size + b, s * blk_size + (b ^ bit_of_core[s % 2])) for s in range(seq_size) for b in range(blk_size)]
    return lax.ppermute(x, ("seq", "blk"), pairs)


def plane_rows(patches):
    rows = patches.shape[0]
    count = rows // 8
    place = lax.broadcasted_iota(jnp.int32, (rows, rows), 0)
    source = lax.broadcasted_iota(jnp.int32, (rows, rows), 1)
    half, plane, window = place // (4 * count), place // count % 4, place % count
    order = (source == 4 * (count * half + window) + plane).astype(BF16)
    return jnp.dot(order, patches, preferred_element_type=F32)


def norm_patches_kernel(patches_ref, gain_ref, first_ref, second_ref, token_ref):
    rows = patches_ref.shape[0]
    normed = normalize(plane_rows(patches_ref[...]), gain_ref[...]).astype(BF16)
    first_ref[...] = normed[: rows // 2]
    second_ref[...] = normed[rows // 2 :]
    token_ref[...] = jnp.zeros_like(token_ref)


def start_copies(pairs, sems):
    copies = [pltpu.make_async_copy(source, goal, sems.at[at]) for at, (source, goal) in enumerate(pairs)]
    for copy in copies:
        copy.start()
    return copies


def same_kernel(*refs):
    pass


def after(x, before):
    return call(same_kernel, "after", like(x), (x, before), aliases={0: 0}, stored=(1,))


def feed_forward(rows, pieces):
    def pre(piece):
        up, bias, _ = piece
        product = up_project(rows, up())
        return product if bias is None else product + bias()

    total, ready = None, pre(pieces[0])
    for at, (_, _, down) in enumerate(pieces):
        later = pre(pieces[at + 1]) if at + 1 < len(pieces) else None
        part = jnp.dot(gelu(ready).astype(BF16), down(), preferred_element_type=F32)
        total = part if total is None else total + part
        ready = later
    return total


def vision_pieces(up, bias, down):
    pieces = []
    tile = up.shape[0] // 2
    for at in (0, tile):
        cut = pl.ds(at, tile)
        pieces.append(
            (
                functools.partial(lambda ref, cut: ref[cut, :], up, cut),
                functools.partial(lambda ref, cut: ref[cut], bias, cut),
                functools.partial(lambda ref, cut: ref[cut, :], down, cut),
            )
        )
    return pieces


def first_kernel(rows_ref, ua, ba, da, ub, bb, db, *refs):
    out_ref, token_ref, da_out, ub_out, db_out, sems = refs
    copies = start_copies([(da, da_out), (ub, ub_out), (db, db_out)], sems)
    rows = rows_ref[...]
    copies[0].wait()
    total = feed_forward(rows, vision_pieces(ua, ba, da_out))
    for copy in copies[1:]:
        copy.wait()
    total = total + feed_forward(rows, vision_pieces(ub_out, bb, db_out))
    out_ref[...] = total.astype(BF16)
    token_ref[...] = jnp.zeros_like(token_ref)


def pass_on(core_ref, ref, out_ref, sem):
    half = out_ref.shape[0]
    for core in range(2):

        @pl.when(core_ref[0] == core)
        def _():
            copy = pltpu.make_async_copy(ref.at[pl.ds(core * half, half)], out_ref, sem)
            copy.start()
            copy.wait()


def second_kernel(core_ref, rows_ref, ua, ba, da, ub, bb, db, before_ref, *refs):
    if len(refs) > 2:
        side_ref, _, half_ref, out_ref, token_ref, sems = refs
        pass_on(core_ref, side_ref, half_ref, sems.at[0])
    else:
        out_ref, token_ref = refs
    total = feed_forward(rows_ref[...], vision_pieces(ua, ba, da) + vision_pieces(ub, bb, db))
    out_ref[...] = total.astype(BF16)
    token_ref[...] = jnp.zeros_like(token_ref)


def own_kernel(first_ref, second_ref, ua, ba, da, ub, bb, db, before_ref, back_ref, proj, out_ref, proj_out, sems):
    copies = start_copies([(proj, proj_out)], sems)
    half = first_ref.shape[0]
    rows = jnp.concatenate([first_ref[...], second_ref[...]], axis=0)
    total = feed_forward(rows, vision_pieces(ua, ba, da) + vision_pieces(ub, bb, db))
    out_ref[pl.ds(0, half), :] = total[:half] + back_ref[...].astype(F32)
    out_ref[pl.ds(half, half), :] = total[half:]
    for copy in copies:
        copy.wait()


def merge_kernel(core_ref, patches_ref, own_ref, back_ref, gain_ref, proj_ref, place_ref, where_ref, *refs):
    if len(refs) > 1:
        side_ref, _, half_ref, out_ref, sems = refs
        pass_on(core_ref, side_ref, half_ref, sems.at[0])
    else:
        out_ref = refs[0]
    rows, width = patches_ref.shape
    count = rows // 8
    wide = plane_rows(patches_ref[...])
    merged = None
    for plane in range(4):
        halves = []
        for half in range(2):
            here = 4 * count * half + plane * count
            vis_out = wide[here : here + count] + own_ref[pl.ds(here, count), :]
            if half:
                vis_out = vis_out + back_ref[pl.ds(plane * count, count), :].astype(F32)
            halves.append(normalize(vis_out, gain_ref[...]).astype(BF16))
        proj = proj_ref[pl.ds(plane * width, width), :]
        part = jnp.dot(jnp.concatenate(halves, axis=0), proj, preferred_element_type=F32)
        merged = part if merged is None else merged + part
    placed = jnp.dot(place_ref[...], merged.astype(BF16), preferred_element_type=F32)
    out_ref[:, :width] = placed.astype(BF16)
    out_ref[:, width:] = where_ref[...]


def place_text_rows(which, capacity, embed_ref, got_ref):
    width = embed_ref.shape[1]
    where = got_ref[:, width:].astype(F32)
    token = lax.broadcasted_iota(jnp.int32, where.shape, 1).astype(F32)
    side_of = lax.broadcasted_iota(jnp.int32, where.shape, 0) // capacity % 2
    pick = ((where == token) & (side_of == which)).astype(F32).astype(BF16)
    by_token = (((0,), (0,)), ((), ()))
    picked = lax.dot_general(pick, got_ref[:, :width], by_token, preferred_element_type=F32)
    taken = lax.dot_general(pick, jnp.ones((pick.shape[0], 128), BF16), by_token, preferred_element_type=F32)
    return jnp.where(taken[:, :1] > 0.5, picked, embed_ref[...].astype(F32))


def joined_kernel(up_ref, down_ref, before_ref, embed_ref, out_ref):
    half = up_ref.shape[0]
    out_ref[pl.ds(0, half), :] = up_ref[...]
    out_ref[pl.ds(half, half), :] = down_ref[...]


def text_pieces(slices):
    return [
        (functools.partial(lambda ref: ref[...], up), None, functools.partial(lambda ref: ref[...], down))
        for up, down in slices
    ]


def across_pieces(halves):
    half = halves[0].shape[0] // 2
    up, down = pl.ds(0, half), pl.ds(half, half)
    return [
        (
            functools.partial(lambda ref: ref[up, :], ref),
            None,
            functools.partial(lambda ref: ref[down, :], ref),
        )
        for ref in halves
    ]


def loaded_pieces(refs, up, down, sems):
    copies = start_copies(
        [(ref, (up, down)[at % 2].at[at // 2]) for at, ref in enumerate(refs)], sems
    )

    def read(at):
        copies[at].wait()
        return (up, down)[at % 2][at // 2]

    return [
        (functools.partial(read, at), None, functools.partial(read, at + 1)) for at in range(0, len(refs), 2)
    ]


def theirs_kernel(capacity, embed_ref, got_ref, gain_ref, *refs):
    slices, (normed_ref, total_ref), scratch = refs[:6], refs[6:8], refs[8:]
    pieces = loaded_pieces(slices, *scratch)
    text_rows = place_text_rows(1, capacity, embed_ref, got_ref)
    normed = normalize(text_rows, gain_ref[...]).astype(BF16)
    normed_ref[...] = normed
    total_ref[...] = feed_forward(normed, pieces)


def theirs_last_kernel(normed_ref, total_ref, *refs):
    pieces = across_pieces(refs[:-1])
    refs[-1][...] = (total_ref[...] + feed_forward(normed_ref[...], pieces)).astype(BF16)


def mine_kernel(capacity, embed_ref, got_ref, gain_ref, *refs):
    slices, halves, out_ref, scratch = refs[:6], refs[6:8], refs[8], refs[9:]
    pieces = loaded_pieces(slices, *scratch)
    text_rows = place_text_rows(0, capacity, embed_ref, got_ref)
    normed = normalize(text_rows, gain_ref[...]).astype(BF16)
    out_ref[...] = text_rows + feed_forward(normed, across_pieces(halves) + pieces)


def per_device(
    patches,
    vis_gain,
    vis_up,
    vis_bias,
    vis_down,
    merge_gain,
    merge_proj,
    text_embed,
    slot_index,
    text_gain,
    text_up,
    text_down,
):
    cycle_size = lax.axis_size("blk")
    merged_count = slot_index.shape[0]
    token_count, width = text_embed.shape
    patch_count = patches.shape[0]
    capacity = 2 * merged_count // cycle_size
    paired = cycle_size == 8
    sides = 2 if paired else 1

    target = slot_index // token_count % cycle_size
    position = slot_index % token_count
    one_hot = (target[:, None] == jnp.arange(cycle_size, dtype=jnp.int32)[None, :]).astype(jnp.int32)
    rank = jnp.sum((jnp.cumsum(one_hot, axis=0) - one_hot) * one_hot, axis=1)
    sent = jnp.arange(cycle_size * sides * capacity, dtype=jnp.int32)[:, None]
    owner = sent // (sides * capacity) ^ (4 * (sent // capacity % sides))
    chosen = (target[None, :] == owner) & (rank[None, :] == sent % capacity)
    place = chosen.astype(BF16)
    where = jnp.max(jnp.where(chosen, position[None, :], -1), axis=1, keepdims=True)
    where = jnp.broadcast_to(where.astype(BF16), (where.shape[0], 128))

    core = (lax.axis_index("seq") % 2).reshape(1)
    half_rows = jax.ShapeDtypeStruct((patch_count // 2, width), BF16)
    far_up, far_down = swap(vis_up, "seq", 1), swap(vis_down, "seq", 1)
    other_bias = swap(after(vis_bias, far_up), "seq", 1)
    first, second, _ = call(
        norm_patches_kernel, "norm_patches", (half_rows, half_rows, TOKEN), (patches, vis_gain)
    )
    far_first, far_second = swap(first, "seq", 2), swap(second, "seq", 2)
    args = (far_first, vis_up, vis_bias, vis_down, far_up, other_bias, far_down)
    outs = (half_rows, TOKEN, like(vis_down), like(vis_up), like(vis_down))
    if paired:
        side_up, side_down = swap_by_core(text_up, (1, 2)), swap_by_core(text_down, (1, 2))
    part_first, first_done, near_down, far_up, far_down = call(
        first_kernel, "vision_first", outs, args, stored=(3, 4, 6), copies=3
    )
    weights = (vis_up, vis_bias, near_down, far_up, other_bias, far_down)
    back_first = swap(part_first, "seq", 2)
    if paired:
        other_embed = swap(text_embed, "blk", 4)
    args = (core, far_second, *weights, first_done)
    outs = (half_rows, TOKEN)
    half_slice = jax.ShapeDtypeStruct((text_up.shape[0] // 2, width), BF16)
    if paired:
        side_up, across_up, part_second, second_done = call(
            second_kernel,
            "vision_second",
            (like(side_up), half_slice, *outs),
            args + (side_up,),
            aliases={len(args): 0},
            copies=1,
            scalars=1,
            microseconds=30,
        )
        other_up, across_up = swap(side_up, "seq", 1), swap_by_core(across_up, (2, 1))
    else:
        part_second, second_done = call(second_kernel, "vision_second", outs, args, scalars=1, microseconds=30)
    back_second = swap(part_second, "seq", 2)
    own_rows = jax.ShapeDtypeStruct((patch_count, width), F32)
    own, merge_proj = call(
        own_kernel,
        "vision_own",
        (own_rows, like(merge_proj)),
        (first, second, *weights, second_done, back_first, merge_proj),
        stored=(10,),
        copies=1,
    )
    args = (core, patches, own, back_second, merge_gain, merge_proj, place, where)
    sent_rows = jax.ShapeDtypeStruct((place.shape[0], width + 128), BF16)
    if paired:
        side_down, across_down, send = call(
            merge_kernel,
            "merge_rows",
            (like(side_down), half_slice, sent_rows),
            args + (side_down,),
            aliases={len(args): 0},
            copies=1,
            scalars=1,
        )
        other_down, across_down = swap(side_down, "seq", 1), swap_by_core(across_down, (2, 1))
    else:
        send = call(merge_kernel, "merge_rows", sent_rows, args, scalars=1)
    got = lax.all_to_all(send, "blk", split_axis=0, concat_axis=0, tiled=True)
    if paired:
        across = call(joined_kernel, "join_across", like(text_up), (across_up, across_down, send, other_embed), stored=(2,), microseconds=20)
        halves = (across, swap(across, "seq", 1))
        other_up, other_down = call(
            same_kernel,
            "hold",
            (like(other_up), like(other_down)),
            (other_up, other_down),
            aliases={0: 0, 1: 1},
            stored=(0, 1),
            microseconds=20,
        )
        slices = (text_up, text_down, side_up, side_down, other_up, other_down)
        room = tuple(pltpu.VMEM((3, *text_up.shape), BF16) for _ in range(2))
        tokens = jax.ShapeDtypeStruct((token_count, width), F32)
        text_normed, total = call(
            functools.partial(theirs_kernel, capacity),
            "text_theirs",
            (like(text_embed), tokens),
            (other_embed, got, text_gain, *slices),
            stored=tuple(range(3, 9)),
            copies=6,
            scratch=room,
            megabytes=20,
        )
        theirs = call(theirs_last_kernel, "text_theirs_last", like(text_embed), (text_normed, total, *halves))
        mine = call(
            functools.partial(mine_kernel, capacity),
            "text_mine",
            tokens,
            (text_embed, got, text_gain, *slices, *halves),
            stored=tuple(range(3, 9)),
            copies=6,
            scratch=room,
            megabytes=20,
        )
        return (mine + swap(theirs, "blk", 4).astype(F32)).astype(BF16)
    tokens = jnp.arange(token_count, dtype=jnp.int32).astype(BF16)
    pick = (got[:, width:][:, :1] == tokens[None, :]).astype(BF16)
    picked = lax.dot_general(pick, got[:, :width], (((0,), (0,)), ((), ())), preferred_element_type=F32)
    taken = jnp.sum(pick.astype(F32), axis=0)[:, None] > 0.5
    text_rows = jnp.where(taken, picked, text_embed.astype(F32))
    text_normed = normalize(text_rows, text_gain).astype(BF16)
    gathered_tokens = lax.all_gather(text_normed, "blk", axis=0, tiled=True)
    hidden = gelu(up_project(gathered_tokens, text_up)).astype(BF16)
    text_mlp = lax.psum_scatter(
        jnp.dot(hidden, text_down, preferred_element_type=F32).astype(BF16),
        "blk",
        scatter_dimension=0,
        tiled=True,
    ).astype(F32)
    return (text_rows + text_mlp).astype(BF16)


def solution(mesh):
    placed = (
        P(("seq", "blk"), None),
        P(),
        P("seq", None),
        P("seq"),
        P("seq", None),
        P(),
        P(),
        P(("seq", "blk"), None),
        P(("seq", "blk")),
        P(),
        P("blk", None),
        P("blk", None),
    )
    return jax.shard_map(
        per_device, mesh=mesh, in_specs=placed, out_specs=P(("seq", "blk"), None), check_vma=False
    )
```

```python
import functools

import jax
import jax.numpy as jnp
from jax import lax
from jax.experimental import pallas as pl
from jax.experimental.pallas import tpu as pltpu
from jax.sharding import PartitionSpec as P

F32 = jnp.float32
BF16 = jnp.bfloat16
VMEM = pl.BlockSpec(memory_space=pltpu.VMEM)
STORED = pl.BlockSpec(memory_space=pltpu.HBM)
SMEM = pl.BlockSpec(memory_space=pltpu.SMEM)
TOKEN = jax.ShapeDtypeStruct((8, 128), F32)


def like(x):
    return jax.ShapeDtypeStruct(x.shape, x.dtype)


def cost(microseconds):
    return pl.CostEstimate(flops=int(microseconds * 1e9), bytes_accessed=1000, transcendentals=0)


def call(kernel, name, out_shape, args, microseconds=0.001, aliases=None, scalars=0, stored=(), copies=0, scratch=(), megabytes=16):
    aliases = aliases or {}
    stored = (*stored, *aliases)
    specs = [SMEM] * scalars + [STORED if at in stored else VMEM for at in range(scalars, len(args))]
    single = not isinstance(out_shape, tuple)
    out_shape = (out_shape,) if single else out_shape
    outs = pl.pallas_call(
        kernel,
        out_shape=out_shape,
        in_specs=specs,
        out_specs=tuple(STORED if at in aliases.values() else VMEM for at in range(len(out_shape))),
        input_output_aliases=aliases,
        scratch_shapes=[*scratch, *([pltpu.SemaphoreType.DMA((copies,))] if copies else [])],
        compiler_params=pltpu.CompilerParams(vmem_limit_bytes=megabytes * 1024 * 1024),
        cost_estimate=cost(microseconds),
        name=name,
    )(*args)
    return outs[0] if single else outs


def normalize(values, row_gain):
    values = values.astype(F32)
    center = values - jnp.mean(values, axis=-1, keepdims=True)
    spread = jnp.mean(center * center, axis=-1, keepdims=True)
    return center * lax.rsqrt(spread + 1e-06) * row_gain


def gelu(v):
    half = 0.5 * v
    return half + half * jnp.tanh(v * (0.7978845608028654 + 0.035677408136300125 * (v * v)))


def up_project(rows_in, up_piece):
    return lax.dot_general(rows_in, up_piece, (((1,), (1,)), ((), ())), preferred_element_type=F32)


def swap(x, axis, bit):
    size = lax.axis_size(axis)
    return lax.ppermute(x, axis, [(i, i ^ bit) for i in range(size)])


def swap_by_core(x, bit_of_core):
    seq_size, blk_size = lax.axis_size("seq"), lax.axis_size("blk")
    pairs = [(s * blk_size + b, s * blk_size + (b ^ bit_of_core[s % 2])) for s in range(seq_size) for b in range(blk_size)]
    return lax.ppermute(x, ("seq", "blk"), pairs)


def plane_rows(patches):
    rows = patches.shape[0]
    count = rows // 8
    place = lax.broadcasted_iota(jnp.int32, (rows, rows), 0)
    source = lax.broadcasted_iota(jnp.int32, (rows, rows), 1)
    half, plane, window = place // (4 * count), place // count % 4, place % count
    order = (source == 4 * (count * half + window) + plane).astype(BF16)
    return jnp.dot(order, patches, preferred_element_type=F32)


def norm_patches_kernel(patches_ref, gain_ref, first_ref, second_ref, token_ref):
    rows = patches_ref.shape[0]
    normed = normalize(plane_rows(patches_ref[...]), gain_ref[...]).astype(BF16)
    first_ref[...] = normed[: rows // 2]
    second_ref[...] = normed[rows // 2 :]
    token_ref[...] = jnp.zeros_like(token_ref)


def start_copies(pairs, sems):
    copies = [pltpu.make_async_copy(source, goal, sems.at[at]) for at, (source, goal) in enumerate(pairs)]
    for copy in copies:
        copy.start()
    return copies


def same_kernel(*refs):
    pass


def after(x, before, microseconds=0.001):
    return call(same_kernel, "after", like(x), (x, before), microseconds=microseconds, aliases={0: 0}, stored=(1,))


def feed_forward(rows, pieces):
    def pre(piece):
        up, bias, _ = piece
        product = up_project(rows, up())
        return product if bias is None else product + bias()

    total, ready = None, pre(pieces[0])
    for at, (_, _, down) in enumerate(pieces):
        later = pre(pieces[at + 1]) if at + 1 < len(pieces) else None
        part = jnp.dot(gelu(ready).astype(BF16), down(), preferred_element_type=F32)
        total = part if total is None else total + part
        ready = later
    return total


def vision_pieces(up, bias, down):
    pieces = []
    tile = up.shape[0] // 2
    for at in (0, tile):
        cut = pl.ds(at, tile)
        pieces.append(
            (
                functools.partial(lambda ref, cut: ref[cut, :], up, cut),
                functools.partial(lambda ref, cut: ref[cut], bias, cut),
                functools.partial(lambda ref, cut: ref[cut, :], down, cut),
            )
        )
    return pieces


def bring_kernel(ua, da, before_ref, ua_out, da_out, sems):
    for copy in start_copies([(ua, ua_out), (da, da_out)], sems):
        copy.wait()


def first_kernel(rows_ref, ua, ba, da, ub, bb, db, out_ref, token_ref, ub_out, db_out, sems):
    copies = start_copies([(ub, ub_out), (db, db_out)], sems)

    def far(at, ref, cut):
        def there():
            if cut.start == 0:
                copies[at].wait()
            return ref[cut, :]

        return there

    tile = ua.shape[0] // 2
    pieces = vision_pieces(ua, ba, da)
    for first in (0, tile):
        cut = pl.ds(first, tile)
        pieces.append((far(0, ub_out, cut), functools.partial(lambda cut: bb[cut], cut), far(1, db_out, cut)))
    out_ref[...] = feed_forward(rows_ref[...], pieces).astype(BF16)
    token_ref[...] = jnp.zeros_like(token_ref)


def pass_on(core_ref, ref, out_ref, sem):
    half = out_ref.shape[0]
    first = pl.multiple_of(core_ref[0] * half, half)
    return start_copies([(ref.at[pl.ds(first, half)], out_ref)], sem)


def pass_kernel(core_ref, side_ref, *refs):
    half_ref, sems = refs[-2:]
    for copy in pass_on(core_ref, side_ref, half_ref, sems):
        copy.wait()


def second_kernel(core_ref, rows_ref, ua, ba, da, ub, bb, db, before_ref, *refs):
    if len(refs) > 2:
        side_ref, embed_ref, _, half_ref, embed_out_ref, out_ref, token_ref, sems = refs
        copies = pass_on(core_ref, side_ref, half_ref, sems)
        embed_out_ref[...] = embed_ref[...]
    else:
        out_ref, token_ref = refs
        copies = ()
    total = feed_forward(rows_ref[...], vision_pieces(ua, ba, da) + vision_pieces(ub, bb, db))
    out_ref[...] = total.astype(BF16)
    token_ref[...] = jnp.zeros_like(token_ref)
    for copy in copies:
        copy.wait()


def own_kernel(first_ref, second_ref, ua, ba, da, ub, bb, db, before_ref, back_ref, proj, out_ref, proj_out, sems):
    copies = start_copies([(proj, proj_out)], sems)
    half = first_ref.shape[0]
    rows = jnp.concatenate([first_ref[...], second_ref[...]], axis=0)
    total = feed_forward(rows, vision_pieces(ua, ba, da) + vision_pieces(ub, bb, db))
    out_ref[pl.ds(0, half), :] = total[:half] + back_ref[...].astype(F32)
    out_ref[pl.ds(half, half), :] = total[half:]
    for copy in copies:
        copy.wait()


def merge_kernel(patches_ref, own_ref, back_ref, gain_ref, proj_ref, place_ref, where_ref, out_ref):
    rows, width = patches_ref.shape
    count = rows // 8
    wide = plane_rows(patches_ref[...])
    merged = None
    for plane in range(4):
        halves = []
        for half in range(2):
            here = 4 * count * half + plane * count
            vis_out = wide[here : here + count] + own_ref[pl.ds(here, count), :]
            if half:
                vis_out = vis_out + back_ref[pl.ds(plane * count, count), :].astype(F32)
            halves.append(normalize(vis_out, gain_ref[...]).astype(BF16))
        proj = proj_ref[pl.ds(plane * width, width), :]
        part = jnp.dot(jnp.concatenate(halves, axis=0), proj, preferred_element_type=F32)
        merged = part if merged is None else merged + part
    placed = jnp.dot(place_ref[...], merged.astype(BF16), preferred_element_type=F32)
    out_ref[:, :width] = placed.astype(BF16)
    out_ref[:, width:] = where_ref[...]


def place_text_rows(which, capacity, embed, got):
    width = embed.shape[1]
    where = got[:, width:].astype(F32)
    token = lax.broadcasted_iota(jnp.int32, where.shape, 1).astype(F32)
    side_of = lax.broadcasted_iota(jnp.int32, where.shape, 0) // capacity % 2
    pick = ((where == token) & (side_of == which)).astype(F32).astype(BF16)
    by_token = (((0,), (0,)), ((), ()))
    picked = lax.dot_general(pick, got[:, :width], by_token, preferred_element_type=F32)
    taken = lax.dot_general(pick, jnp.ones((pick.shape[0], 128), BF16), by_token, preferred_element_type=F32)
    return jnp.where(taken[:, :1] > 0.5, picked, embed.astype(F32))


def load_text(rows, slices, halves, rooms, up, down, sems):
    half = up.shape[1] // 2
    pairs = list(zip(rows, rooms))
    waits = []
    for at in range(3):
        for ref, room in ((slices[2 * at], up), (slices[2 * at + 1], down)):
            waits.append([len(pairs)])
            pairs.append((ref, room.at[at]))
    for at, room in enumerate((up, down)):
        if halves:
            waits.append([len(pairs), len(pairs) + 1])
        for number, ref in enumerate(halves[2 * at : 2 * at + 2]):
            pairs.append((ref, room.at[3, pl.ds(number * half, half)]))
    copies = start_copies(pairs, sems)

    def read(at):
        for number in waits[at]:
            copies[number].wait()
        return (up, down)[at % 2][at // 2]

    pieces = [(functools.partial(read, at), None, functools.partial(read, at + 1)) for at in range(0, len(waits), 2)]
    for copy in copies[: len(rows)]:
        copy.wait()
    return pieces


def theirs_kernel(capacity, embed_ref, got_ref, *refs):
    slices, gain_ref, normed_ref, total_ref = refs[:6], refs[6], refs[7], refs[8]
    embed, got, up, down, sems = refs[9:]
    pieces = load_text((embed_ref, got_ref), slices, (), (embed, got), up, down, sems)
    text_rows = place_text_rows(1, capacity, embed[...], got[...])
    normed = normalize(text_rows, gain_ref[...]).astype(BF16)
    normed_ref[...] = normed
    total_ref[...] = feed_forward(normed, pieces)


def theirs_last_kernel(normed_ref, total_ref, up_ref, other_up_ref, down_ref, other_down_ref, out_ref):
    def both(mine_ref, other_ref):
        return lambda: jnp.concatenate([mine_ref[...], other_ref[...]], axis=0)

    total = feed_forward(normed_ref[...], [(both(up_ref, other_up_ref), None, both(down_ref, other_down_ref))])
    out_ref[...] = (total_ref[...] + total).astype(BF16)


def mine_kernel(capacity, embed_ref, got_ref, *refs):
    slices, halves, gain_ref, out_ref = refs[:6], refs[6:10], refs[10], refs[11]
    embed, got, up, down, sems = refs[12:]
    pieces = load_text((embed_ref, got_ref), slices, halves, (embed, got), up, down, sems)
    text_rows = place_text_rows(0, capacity, embed[...], got[...])
    out_ref[...] = text_rows + feed_forward(normalize(text_rows, gain_ref[...]).astype(BF16), pieces)


def per_device(
    patches,
    vis_gain,
    vis_up,
    vis_bias,
    vis_down,
    merge_gain,
    merge_proj,
    text_embed,
    slot_index,
    text_gain,
    text_up,
    text_down,
):
    cycle_size = lax.axis_size("blk")
    merged_count = slot_index.shape[0]
    token_count, width = text_embed.shape
    patch_count = patches.shape[0]
    capacity = 2 * merged_count // cycle_size
    paired = cycle_size == 8
    sides = 2 if paired else 1

    target = slot_index // token_count % cycle_size
    position = slot_index % token_count
    one_hot = (target[:, None] == jnp.arange(cycle_size, dtype=jnp.int32)[None, :]).astype(jnp.int32)
    rank = jnp.sum((jnp.cumsum(one_hot, axis=0) - one_hot) * one_hot, axis=1)
    sent = jnp.arange(cycle_size * sides * capacity, dtype=jnp.int32)[:, None]
    owner = sent // (sides * capacity) ^ (4 * (sent // capacity % sides))
    chosen = (target[None, :] == owner) & (rank[None, :] == sent % capacity)
    place = chosen.astype(BF16)
    where = jnp.max(jnp.where(chosen, position[None, :], -1), axis=1, keepdims=True)
    where = jnp.broadcast_to(where.astype(BF16), (where.shape[0], 128))

    core = (lax.axis_index("seq") % 2).reshape(1)
    half_rows = jax.ShapeDtypeStruct((patch_count // 2, width), BF16)
    far_up, far_down = swap(vis_up, "seq", 1), swap(vis_down, "seq", 1)
    other_bias = swap(after(vis_bias, far_up), "seq", 1)
    first, second, normed = call(
        norm_patches_kernel, "norm_patches", (half_rows, half_rows, TOKEN), (patches, vis_gain), megabytes=40
    )
    far_first, far_second = swap(first, "seq", 2), swap(second, "seq", 2)
    near_up, near_down = call(
        bring_kernel,
        "bring_vision",
        (like(vis_up), like(vis_down)),
        (vis_up, vis_down, normed),
        stored=(0, 1),
        copies=2,
        megabytes=44,
    )
    args = (far_first, near_up, vis_bias, near_down, far_up, other_bias, far_down)
    outs = (half_rows, TOKEN, like(vis_up), like(vis_down))
    if paired:
        side_up, side_down = swap_by_core(text_up, (1, 2)), swap_by_core(text_down, (1, 2))
    part_first, first_done, far_up, far_down = call(
        first_kernel, "vision_first", outs, args, stored=(4, 6), copies=2, megabytes=36
    )
    weights = (near_up, vis_bias, near_down, far_up, other_bias, far_down)
    back_first = swap(part_first, "seq", 2)
    args = (core, far_second, *weights, first_done)
    outs = (half_rows, TOKEN)
    half_slice = jax.ShapeDtypeStruct((text_up.shape[0] // 2, width), BF16)
    if paired:
        side_up, across_up, other_embed, part_second, second_done = call(
            second_kernel,
            "vision_second",
            (like(side_up), half_slice, like(text_embed), *outs),
            args + (side_up, text_embed),
            aliases={len(args): 0},
            copies=1,
            scalars=1,
            microseconds=30,
        )
        other_up, across_up = swap(side_up, "seq", 1), swap_by_core(across_up, (2, 1))
        other_embed = swap(other_embed, "blk", 4)
    else:
        part_second, second_done = call(second_kernel, "vision_second", outs, args, scalars=1, microseconds=30)
    back_second = swap(part_second, "seq", 2)
    own_rows = jax.ShapeDtypeStruct((patch_count, width), F32)
    own, merge_proj = call(
        own_kernel,
        "vision_own",
        (own_rows, like(merge_proj)),
        (first, second, *weights, second_done, back_first, merge_proj),
        stored=(10,),
        microseconds=5,
        copies=1,
    )
    sent_rows = jax.ShapeDtypeStruct((place.shape[0], width + 128), BF16)
    args = (patches, own, back_second, merge_gain, merge_proj, place, where)
    send = call(merge_kernel, "merge_rows", sent_rows, args)
    if paired:
        side_down, across_up, across_down = call(
            pass_kernel,
            "pass_down",
            (like(side_down), like(across_up), half_slice),
            (core, side_down, send, across_up, other_embed),
            aliases={1: 0, 3: 1},
            scalars=1,
            stored=(2, 3, 4),
            copies=1,
            microseconds=0.001,
        )
        other_down, across_down = swap(side_down, "seq", 1), swap_by_core(across_down, (2, 1))
    got = lax.all_to_all(send, "blk", split_axis=0, concat_axis=0, tiled=True)
    if paired:
        got = after(got, send, microseconds=5)
        slices = (text_up, text_down, side_up, side_down, other_up, other_down)
        room = (
            pltpu.VMEM(text_embed.shape, BF16),
            pltpu.VMEM(got.shape, BF16),
            pltpu.VMEM((4, *text_up.shape), BF16),
            pltpu.VMEM((4, *text_up.shape), BF16),
        )
        sums = jax.ShapeDtypeStruct((token_count, width), F32)
        text_normed, total = call(
            functools.partial(theirs_kernel, capacity),
            "text_theirs",
            (like(text_embed), sums),
            (other_embed, got, *slices, text_gain),
            stored=tuple(range(8)),
            copies=8,
            scratch=room,
            megabytes=24,
        )
        across_down = after(across_down, text_normed)
        halves = (across_up, swap(across_up, "seq", 1), across_down, swap(across_down, "seq", 1))
        theirs = call(theirs_last_kernel, "text_theirs_last", like(text_embed), (text_normed, total, *halves))
        mine = call(
            functools.partial(mine_kernel, capacity),
            "text_mine",
            sums,
            (text_embed, got, *slices, *halves, text_gain),
            stored=tuple(range(12)),
            copies=12,
            scratch=room,
            megabytes=24,
        )
        return (mine + swap(theirs, "blk", 4).astype(F32)).astype(BF16)
    tokens = jnp.arange(token_count, dtype=jnp.int32).astype(BF16)
    pick = (got[:, width:][:, :1] == tokens[None, :]).astype(BF16)
    picked = lax.dot_general(pick, got[:, :width], (((0,), (0,)), ((), ())), preferred_element_type=F32)
    taken = jnp.sum(pick.astype(F32), axis=0)[:, None] > 0.5
    text_rows = jnp.where(taken, picked, text_embed.astype(F32))
    text_normed = normalize(text_rows, text_gain).astype(BF16)
    gathered_tokens = lax.all_gather(text_normed, "blk", axis=0, tiled=True)
    hidden = gelu(up_project(gathered_tokens, text_up)).astype(BF16)
    text_mlp = lax.psum_scatter(
        jnp.dot(hidden, text_down, preferred_element_type=F32).astype(BF16),
        "blk",
        scatter_dimension=0,
        tiled=True,
    ).astype(F32)
    return (text_rows + text_mlp).astype(BF16)


def solution(mesh):
    placed = (
        P(("seq", "blk"), None),
        P(),
        P("seq", None),
        P("seq"),
        P("seq", None),
        P(),
        P(),
        P(("seq", "blk"), None),
        P(("seq", "blk")),
        P(),
        P("blk", None),
        P("blk", None),
    )
    return jax.shard_map(
        per_device, mesh=mesh, in_specs=placed, out_specs=P(("seq", "blk"), None), check_vma=False
    )
```

```python
import functools

import jax
import jax.numpy as jnp
from jax import lax
from jax.experimental import pallas as pl
from jax.experimental.pallas import tpu as pltpu
from jax.sharding import PartitionSpec as P

F32 = jnp.float32
BF16 = jnp.bfloat16
VMEM = pl.BlockSpec(memory_space=pltpu.VMEM)
STORED = pl.BlockSpec(memory_space=pltpu.HBM)
SMEM = pl.BlockSpec(memory_space=pltpu.SMEM)
TOKEN = jax.ShapeDtypeStruct((8, 128), F32)


def like(x):
    return jax.ShapeDtypeStruct(x.shape, x.dtype)


def cost(microseconds):
    return pl.CostEstimate(flops=int(microseconds * 1e9), bytes_accessed=1000, transcendentals=0)


def call(kernel, name, out_shape, args, microseconds=0.001, aliases=None, scalars=0, stored=(), copies=0, scratch=(), megabytes=16):
    aliases = aliases or {}
    stored = (*stored, *aliases)
    specs = [SMEM] * scalars + [STORED if at in stored else VMEM for at in range(scalars, len(args))]
    single = not isinstance(out_shape, tuple)
    out_shape = (out_shape,) if single else out_shape
    outs = pl.pallas_call(
        kernel,
        out_shape=out_shape,
        in_specs=specs,
        out_specs=tuple(STORED if at in aliases.values() else VMEM for at in range(len(out_shape))),
        input_output_aliases=aliases,
        scratch_shapes=[*scratch, *([pltpu.SemaphoreType.DMA((copies,))] if copies else [])],
        compiler_params=pltpu.CompilerParams(vmem_limit_bytes=megabytes * 1024 * 1024),
        cost_estimate=cost(microseconds),
        name=name,
    )(*args)
    return outs[0] if single else outs


def normalize(values, row_gain):
    values = values.astype(F32)
    center = values - jnp.mean(values, axis=-1, keepdims=True)
    spread = jnp.mean(center * center, axis=-1, keepdims=True)
    return center * lax.rsqrt(spread + 1e-06) * row_gain


def gelu(v):
    half = 0.5 * v
    return half + half * jnp.tanh(v * (0.7978845608028654 + 0.035677408136300125 * (v * v)))


def up_project(rows_in, up_piece):
    return lax.dot_general(rows_in, up_piece, (((1,), (1,)), ((), ())), preferred_element_type=F32)


def swap(x, axis, bit):
    size = lax.axis_size(axis)
    return lax.ppermute(x, axis, [(i, i ^ bit) for i in range(size)])


def swap_by_core(x, bit_of_core):
    seq_size, blk_size = lax.axis_size("seq"), lax.axis_size("blk")
    pairs = [(s * blk_size + b, s * blk_size + (b ^ bit_of_core[s % 2])) for s in range(seq_size) for b in range(blk_size)]
    return lax.ppermute(x, ("seq", "blk"), pairs)


def plane_rows(patches):
    rows = patches.shape[0]
    count = rows // 8
    place = lax.broadcasted_iota(jnp.int32, (rows, rows), 0)
    source = lax.broadcasted_iota(jnp.int32, (rows, rows), 1)
    half, plane, window = place // (4 * count), place // count % 4, place % count
    order = (source == 4 * (count * half + window) + plane).astype(BF16)
    return jnp.dot(order, patches, preferred_element_type=F32)


def norm_patches_kernel(patches_ref, gain_ref, first_ref, second_ref, token_ref):
    rows = patches_ref.shape[0]
    normed = normalize(plane_rows(patches_ref[...]), gain_ref[...]).astype(BF16)
    first_ref[...] = normed[: rows // 2]
    second_ref[...] = normed[rows // 2 :]
    token_ref[...] = jnp.zeros_like(token_ref)


def start_copies(pairs, sems):
    copies = [pltpu.make_async_copy(source, goal, sems.at[at]) for at, (source, goal) in enumerate(pairs)]
    for copy in copies:
        copy.start()
    return copies


def same_kernel(*refs):
    pass


def after(x, before, microseconds=0.001):
    return call(same_kernel, "after", like(x), (x, before), microseconds=microseconds, aliases={0: 0}, stored=(1,))


def feed_forward(rows, pieces):
    def pre(piece):
        up, bias, _ = piece
        product = up_project(rows, up())
        return product if bias is None else product + bias()

    total, ready = None, pre(pieces[0])
    for at, (_, _, down) in enumerate(pieces):
        later = pre(pieces[at + 1]) if at + 1 < len(pieces) else None
        part = jnp.dot(gelu(ready).astype(BF16), down(), preferred_element_type=F32)
        total = part if total is None else total + part
        ready = later
    return total


def vision_pieces(up, bias, down):
    pieces = []
    tile = up.shape[0] // 2
    for at in (0, tile):
        cut = pl.ds(at, tile)
        pieces.append(
            (
                functools.partial(lambda ref, cut: ref[cut, :], up, cut),
                functools.partial(lambda ref, cut: ref[cut], bias, cut),
                functools.partial(lambda ref, cut: ref[cut, :], down, cut),
            )
        )
    return pieces


def bring_kernel(ua, da, before_ref, ua_out, da_out, sems):
    for copy in start_copies([(ua, ua_out), (da, da_out)], sems):
        copy.wait()


def first_kernel(rows_ref, ua, ba, da, ub, bb, db, out_ref, token_ref, ub_out, db_out, sems):
    copies = start_copies([(ub, ub_out), (db, db_out)], sems)

    def far(at, ref, cut):
        def there():
            if cut.start == 0:
                copies[at].wait()
            return ref[cut, :]

        return there

    tile = ua.shape[0] // 2
    pieces = vision_pieces(ua, ba, da)
    for first in (0, tile):
        cut = pl.ds(first, tile)
        pieces.append((far(0, ub_out, cut), functools.partial(lambda cut: bb[cut], cut), far(1, db_out, cut)))
    out_ref[...] = feed_forward(rows_ref[...], pieces).astype(BF16)
    token_ref[...] = jnp.zeros_like(token_ref)


def pass_quarter(place_ref, ref, out_ref, sems):
    quarter = out_ref.shape[0]
    first = pl.multiple_of((2 * place_ref[0] + place_ref[1]) * quarter, quarter)
    return start_copies([(ref.at[pl.ds(first, quarter)], out_ref)], sems)


def order_kernel(place_ref, mine_ref, other_ref, out_ref):
    quarter = mine_ref.shape[0]
    for chip in range(2):
        out_ref[pl.ds(chip * quarter, quarter), :] = jnp.where(place_ref[1] == chip, mine_ref[...], other_ref[...])


def pass_on(core_ref, ref, out_ref, sem):
    half = out_ref.shape[0]
    first = pl.multiple_of(core_ref[0] * half, half)
    return start_copies([(ref.at[pl.ds(first, half)], out_ref)], sem)


def pass_kernel(core_ref, side_ref, *refs):
    half_ref, sems = refs[-2:]
    for copy in pass_on(core_ref, side_ref, half_ref, sems):
        copy.wait()


def second_kernel(core_ref, rows_ref, ua, ba, da, ub, bb, db, before_ref, *refs):
    if len(refs) > 2:
        side_ref, embed_ref, _, half_ref, embed_out_ref, out_ref, token_ref, sems = refs
        copies = pass_quarter(core_ref, side_ref, half_ref, sems)
        embed_out_ref[...] = embed_ref[...]
    else:
        out_ref, token_ref = refs
        copies = ()
    total = feed_forward(rows_ref[...], vision_pieces(ua, ba, da) + vision_pieces(ub, bb, db))
    out_ref[...] = total.astype(BF16)
    token_ref[...] = jnp.zeros_like(token_ref)
    for copy in copies:
        copy.wait()


def own_kernel(first_ref, second_ref, ua, ba, da, ub, bb, db, before_ref, back_ref, proj, out_ref, proj_out, sems):
    copies = start_copies([(proj, proj_out)], sems)
    half = first_ref.shape[0]
    rows = jnp.concatenate([first_ref[...], second_ref[...]], axis=0)
    total = feed_forward(rows, vision_pieces(ua, ba, da) + vision_pieces(ub, bb, db))
    out_ref[pl.ds(0, half), :] = total[:half] + back_ref[...].astype(F32)
    out_ref[pl.ds(half, half), :] = total[half:]
    for copy in copies:
        copy.wait()


def merge_kernel(patches_ref, own_ref, back_ref, gain_ref, proj_ref, place_ref, where_ref, out_ref):
    rows, width = patches_ref.shape
    count = rows // 8
    wide = plane_rows(patches_ref[...])
    merged = None
    for plane in range(4):
        halves = []
        for half in range(2):
            here = 4 * count * half + plane * count
            vis_out = wide[here : here + count] + own_ref[pl.ds(here, count), :]
            if half:
                vis_out = vis_out + back_ref[pl.ds(plane * count, count), :].astype(F32)
            halves.append(normalize(vis_out, gain_ref[...]).astype(BF16))
        proj = proj_ref[pl.ds(plane * width, width), :]
        part = jnp.dot(jnp.concatenate(halves, axis=0), proj, preferred_element_type=F32)
        merged = part if merged is None else merged + part
    placed = jnp.dot(place_ref[...], merged.astype(BF16), preferred_element_type=F32)
    out_ref[:, :width] = placed.astype(BF16)
    out_ref[:, width:] = where_ref[...]


def place_text_rows(which, capacity, embed, got):
    width = embed.shape[1]
    where = got[:, width:].astype(F32)
    token = lax.broadcasted_iota(jnp.int32, where.shape, 1).astype(F32)
    side_of = lax.broadcasted_iota(jnp.int32, where.shape, 0) // capacity % 2
    pick = ((where == token) & (side_of == which)).astype(F32).astype(BF16)
    by_token = (((0,), (0,)), ((), ()))
    picked = lax.dot_general(pick, got[:, :width], by_token, preferred_element_type=F32)
    taken = lax.dot_general(pick, jnp.ones((pick.shape[0], 128), BF16), by_token, preferred_element_type=F32)
    return jnp.where(taken[:, :1] > 0.5, picked, embed.astype(F32))


def load_text(rows, slices, halves, rooms, up, down, sems):
    half = up.shape[1] // 2
    pairs = list(zip(rows, rooms))
    waits = []
    for at in range(3):
        for ref, room in ((slices[2 * at], up), (slices[2 * at + 1], down)):
            waits.append([len(pairs)])
            pairs.append((ref, room.at[at]))
    for at, room in enumerate((up, down)):
        if halves:
            waits.append([len(pairs), len(pairs) + 1])
        for number, ref in enumerate(halves[2 * at : 2 * at + 2]):
            pairs.append((ref, room.at[3, pl.ds(number * half, half)]))
    copies = start_copies(pairs, sems)

    def read(at):
        for number in waits[at]:
            copies[number].wait()
        return (up, down)[at % 2][at // 2]

    pieces = [(functools.partial(read, at), None, functools.partial(read, at + 1)) for at in range(0, len(waits), 2)]
    for copy in copies[: len(rows)]:
        copy.wait()
    return pieces


def theirs_kernel(capacity, embed_ref, got_ref, *refs):
    slices, gain_ref, normed_ref, total_ref = refs[:6], refs[6], refs[7], refs[8]
    embed, got, up, down, sems = refs[9:]
    pieces = load_text((embed_ref, got_ref), slices, (), (embed, got), up, down, sems)
    text_rows = place_text_rows(1, capacity, embed[...], got[...])
    normed = normalize(text_rows, gain_ref[...]).astype(BF16)
    normed_ref[...] = normed
    total_ref[...] = feed_forward(normed, pieces)


def theirs_last_kernel(normed_ref, total_ref, up_ref, other_up_ref, down_ref, other_down_ref, out_ref):
    def both(mine_ref, other_ref):
        return lambda: jnp.concatenate([mine_ref[...], other_ref[...]], axis=0)

    total = feed_forward(normed_ref[...], [(both(up_ref, other_up_ref), None, both(down_ref, other_down_ref))])
    out_ref[...] = (total_ref[...] + total).astype(BF16)


def mine_kernel(capacity, embed_ref, got_ref, *refs):
    slices, halves, gain_ref, out_ref = refs[:6], refs[6:10], refs[10], refs[11]
    embed, got, up, down, sems = refs[12:]
    pieces = load_text((embed_ref, got_ref), slices, halves, (embed, got), up, down, sems)
    text_rows = place_text_rows(0, capacity, embed[...], got[...])
    out_ref[...] = text_rows + feed_forward(normalize(text_rows, gain_ref[...]).astype(BF16), pieces)


def per_device(
    patches,
    vis_gain,
    vis_up,
    vis_bias,
    vis_down,
    merge_gain,
    merge_proj,
    text_embed,
    slot_index,
    text_gain,
    text_up,
    text_down,
):
    cycle_size = lax.axis_size("blk")
    merged_count = slot_index.shape[0]
    token_count, width = text_embed.shape
    patch_count = patches.shape[0]
    capacity = 2 * merged_count // cycle_size
    paired = cycle_size == 8
    sides = 2 if paired else 1

    target = slot_index // token_count % cycle_size
    position = slot_index % token_count
    one_hot = (target[:, None] == jnp.arange(cycle_size, dtype=jnp.int32)[None, :]).astype(jnp.int32)
    rank = jnp.sum((jnp.cumsum(one_hot, axis=0) - one_hot) * one_hot, axis=1)
    sent = jnp.arange(cycle_size * sides * capacity, dtype=jnp.int32)[:, None]
    owner = sent // (sides * capacity) ^ (4 * (sent // capacity % sides))
    chosen = (target[None, :] == owner) & (rank[None, :] == sent % capacity)
    place = chosen.astype(BF16)
    where = jnp.max(jnp.where(chosen, position[None, :], -1), axis=1, keepdims=True)
    where = jnp.broadcast_to(where.astype(BF16), (where.shape[0], 128))

    core = (lax.axis_index("seq") % 2).reshape(1)
    core_and_x = jnp.stack([lax.axis_index("seq") % 2, lax.axis_index("seq") // 2 % 2])
    half_rows = jax.ShapeDtypeStruct((patch_count // 2, width), BF16)
    far_up, far_down = swap(vis_up, "seq", 1), swap(vis_down, "seq", 1)
    other_bias = swap(after(vis_bias, far_up), "seq", 1)
    first, second, normed = call(
        norm_patches_kernel, "norm_patches", (half_rows, half_rows, TOKEN), (patches, vis_gain), megabytes=40
    )
    far_first, far_second = swap(first, "seq", 2), swap(second, "seq", 2)
    near_up, near_down = call(
        bring_kernel,
        "bring_vision",
        (like(vis_up), like(vis_down)),
        (vis_up, vis_down, normed),
        stored=(0, 1),
        copies=2,
        megabytes=44,
    )
    args = (far_first, near_up, vis_bias, near_down, far_up, other_bias, far_down)
    outs = (half_rows, TOKEN, like(vis_up), like(vis_down))
    if paired:
        side_up, side_down = swap_by_core(text_up, (1, 2)), swap_by_core(text_down, (1, 2))
    part_first, first_done, far_up, far_down = call(
        first_kernel, "vision_first", outs, args, stored=(4, 6), copies=2, megabytes=38
    )
    weights = (near_up, vis_bias, near_down, far_up, other_bias, far_down)
    back_first = swap(part_first, "seq", 2)
    args = (core_and_x, far_second, *weights, first_done)
    outs = (half_rows, TOKEN)
    half_slice = jax.ShapeDtypeStruct((text_up.shape[0] // 2, width), BF16)
    quarter_slice = jax.ShapeDtypeStruct((text_up.shape[0] // 4, width), BF16)
    if paired:
        side_up, across_up, other_embed, part_second, second_done = call(
            second_kernel,
            "vision_second",
            (like(side_up), quarter_slice, like(text_embed), *outs),
            args + (side_up, text_embed),
            aliases={len(args): 0},
            copies=1,
            scalars=1,
            microseconds=30,
        )
        other_up, across_up = swap(side_up, "seq", 1), swap_by_core(across_up, (2, 1))
        other_embed = swap(other_embed, "blk", 4)
    else:
        part_second, second_done = call(second_kernel, "vision_second", outs, args, scalars=1, microseconds=30)
    back_second = swap(part_second, "seq", 2)
    own_rows = jax.ShapeDtypeStruct((patch_count, width), F32)
    own, merge_proj = call(
        own_kernel,
        "vision_own",
        (own_rows, like(merge_proj)),
        (first, second, *weights, second_done, back_first, merge_proj),
        stored=(10,),
        microseconds=10,
        copies=1,
    )
    sent_rows = jax.ShapeDtypeStruct((place.shape[0], width + 128), BF16)
    args = (patches, own, back_second, merge_gain, merge_proj, place, where)
    send = call(merge_kernel, "merge_rows", sent_rows, args)
    if paired:
        side_down, across_down = call(
            pass_kernel,
            "pass_down",
            (like(side_down), half_slice),
            (core, side_down, send),
            aliases={1: 0},
            scalars=1,
            stored=(2,),
            copies=1,
            microseconds=0.001,
        )
        other_embed, across_up = call(
            same_kernel,
            "gate",
            (like(other_embed), like(across_up)),
            (other_embed, across_up, send),
            aliases={0: 0, 1: 1},
            stored=(2,),
            microseconds=9,
        )
        across_up = call(
            order_kernel,
            "order_across",
            half_slice,
            (core_and_x, across_up, swap(across_up, "seq", 2)),
            scalars=1,
            microseconds=0.001,
        )
        other_down, across_down = swap(side_down, "seq", 1), swap_by_core(across_down, (2, 1))
    got = lax.all_to_all(send, "blk", split_axis=0, concat_axis=0, tiled=True)
    if paired:
        got = after(got, send, microseconds=6)
        slices = (text_up, text_down, side_up, side_down, other_up, other_down)
        room = (
            pltpu.VMEM(text_embed.shape, BF16),
            pltpu.VMEM(got.shape, BF16),
            pltpu.VMEM((4, *text_up.shape), BF16),
            pltpu.VMEM((4, *text_up.shape), BF16),
        )
        sums = jax.ShapeDtypeStruct((token_count, width), F32)
        text_normed, total = call(
            functools.partial(theirs_kernel, capacity),
            "text_theirs",
            (like(text_embed), sums),
            (other_embed, got, *slices, text_gain),
            stored=tuple(range(8)),
            copies=8,
            scratch=room,
            megabytes=24,
        )
        across_down = after(across_down, text_normed)
        halves = (across_up, swap(across_up, "seq", 1), across_down, swap(across_down, "seq", 1))
        theirs = call(theirs_last_kernel, "text_theirs_last", like(text_embed), (text_normed, total, *halves))
        mine = call(
            functools.partial(mine_kernel, capacity),
            "text_mine",
            sums,
            (text_embed, got, *slices, *halves, text_gain),
            stored=tuple(range(12)),
            copies=12,
            scratch=room,
            megabytes=24,
        )
        return (mine + swap(theirs, "blk", 4).astype(F32)).astype(BF16)
    tokens = jnp.arange(token_count, dtype=jnp.int32).astype(BF16)
    pick = (got[:, width:][:, :1] == tokens[None, :]).astype(BF16)
    picked = lax.dot_general(pick, got[:, :width], (((0,), (0,)), ((), ())), preferred_element_type=F32)
    taken = jnp.sum(pick.astype(F32), axis=0)[:, None] > 0.5
    text_rows = jnp.where(taken, picked, text_embed.astype(F32))
    text_normed = normalize(text_rows, text_gain).astype(BF16)
    gathered_tokens = lax.all_gather(text_normed, "blk", axis=0, tiled=True)
    hidden = gelu(up_project(gathered_tokens, text_up)).astype(BF16)
    text_mlp = lax.psum_scatter(
        jnp.dot(hidden, text_down, preferred_element_type=F32).astype(BF16),
        "blk",
        scatter_dimension=0,
        tiled=True,
    ).astype(F32)
    return (text_rows + text_mlp).astype(BF16)


def solution(mesh):
    placed = (
        P(("seq", "blk"), None),
        P(),
        P("seq", None),
        P("seq"),
        P("seq", None),
        P(),
        P(),
        P(("seq", "blk"), None),
        P(("seq", "blk")),
        P(),
        P("blk", None),
        P("blk", None),
    )
    return jax.shard_map(
        per_device, mesh=mesh, in_specs=placed, out_specs=P(("seq", "blk"), None), check_vma=False
    )
```

```python
import functools

import jax
import jax.numpy as jnp
from jax import lax
from jax.experimental import pallas as pl
from jax.experimental.pallas import tpu as pltpu
from jax.sharding import PartitionSpec as P

F32 = jnp.float32
BF16 = jnp.bfloat16
VMEM = pl.BlockSpec(memory_space=pltpu.VMEM)
STORED = pl.BlockSpec(memory_space=pltpu.HBM)
SMEM = pl.BlockSpec(memory_space=pltpu.SMEM)
TOKEN = jax.ShapeDtypeStruct((8, 128), F32)


def like(x):
    return jax.ShapeDtypeStruct(x.shape, x.dtype)


def cost(microseconds):
    return pl.CostEstimate(flops=int(microseconds * 1e9), bytes_accessed=1000, transcendentals=0)


def call(kernel, name, out_shape, args, microseconds=0.001, aliases=None, scalars=0, stored=(), copies=0, scratch=(), megabytes=16):
    aliases = aliases or {}
    stored = (*stored, *aliases)
    specs = [SMEM] * scalars + [STORED if at in stored else VMEM for at in range(scalars, len(args))]
    single = not isinstance(out_shape, tuple)
    out_shape = (out_shape,) if single else out_shape
    outs = pl.pallas_call(
        kernel,
        out_shape=out_shape,
        in_specs=specs,
        out_specs=tuple(STORED if at in aliases.values() else VMEM for at in range(len(out_shape))),
        input_output_aliases=aliases,
        scratch_shapes=[*scratch, *([pltpu.SemaphoreType.DMA((copies,))] if copies else [])],
        compiler_params=pltpu.CompilerParams(vmem_limit_bytes=megabytes * 1024 * 1024),
        cost_estimate=cost(microseconds),
        name=name,
    )(*args)
    return outs[0] if single else outs


def normalize(values, row_gain):
    values = values.astype(F32)
    center = values - jnp.mean(values, axis=-1, keepdims=True)
    spread = jnp.mean(center * center, axis=-1, keepdims=True)
    return center * lax.rsqrt(spread + 1e-06) * row_gain


def gelu(v):
    half = 0.5 * v
    return half + half * jnp.tanh(v * (0.7978845608028654 + 0.035677408136300125 * (v * v)))


def up_project(rows_in, up_piece):
    return lax.dot_general(rows_in, up_piece, (((1,), (1,)), ((), ())), preferred_element_type=F32)


def swap(x, axis, bit):
    size = lax.axis_size(axis)
    return lax.ppermute(x, axis, [(i, i ^ bit) for i in range(size)])


def swap_by_core(x, bit_of_core):
    seq_size, blk_size = lax.axis_size("seq"), lax.axis_size("blk")
    pairs = [(s * blk_size + b, s * blk_size + (b ^ bit_of_core[s % 2])) for s in range(seq_size) for b in range(blk_size)]
    return lax.ppermute(x, ("seq", "blk"), pairs)


def plane_rows(patches):
    rows = patches.shape[0]
    count = rows // 8
    place = lax.broadcasted_iota(jnp.int32, (rows, rows), 0)
    source = lax.broadcasted_iota(jnp.int32, (rows, rows), 1)
    half, plane, window = place // (4 * count), place // count % 4, place % count
    order = (source == 4 * (count * half + window) + plane).astype(BF16)
    return jnp.dot(order, patches, preferred_element_type=F32)


def norm_patches_kernel(patches_ref, gain_ref, first_ref, second_ref, token_ref):
    rows = patches_ref.shape[0]
    normed = normalize(plane_rows(patches_ref[...]), gain_ref[...]).astype(BF16)
    first_ref[...] = normed[: rows // 2]
    second_ref[...] = normed[rows // 2 :]
    token_ref[...] = jnp.zeros_like(token_ref)


def start_copies(pairs, sems):
    copies = [pltpu.make_async_copy(source, goal, sems.at[at]) for at, (source, goal) in enumerate(pairs)]
    for copy in copies:
        copy.start()
    return copies


def same_kernel(*refs):
    pass


def after(x, before, microseconds=0.001):
    return call(same_kernel, "after", like(x), (x, before), microseconds=microseconds, aliases={0: 0}, stored=(1,))


def feed_forward(rows, pieces):
    def pre(piece):
        up, bias, _ = piece
        product = up_project(rows, up())
        return product if bias is None else product + bias()

    total, ready = None, pre(pieces[0])
    for at, (_, _, down) in enumerate(pieces):
        later = pre(pieces[at + 1]) if at + 1 < len(pieces) else None
        part = jnp.dot(gelu(ready).astype(BF16), down(), preferred_element_type=F32)
        total = part if total is None else total + part
        ready = later
    return total


def vision_pieces(up, bias, down):
    pieces = []
    tile = up.shape[0] // 2
    for at in (0, tile):
        cut = pl.ds(at, tile)
        pieces.append(
            (
                functools.partial(lambda ref, cut: ref[cut, :], up, cut),
                functools.partial(lambda ref, cut: ref[cut], bias, cut),
                functools.partial(lambda ref, cut: ref[cut, :], down, cut),
            )
        )
    return pieces


def bring_kernel(ua, da, before_ref, ua_out, da_out, sems):
    for copy in start_copies([(ua, ua_out), (da, da_out)], sems):
        copy.wait()


def first_kernel(rows_ref, ua, ba, da, ub, bb, db, out_ref, token_ref, ub_out, db_out, sems):
    copies = start_copies([(ub, ub_out), (db, db_out)], sems)

    def far(at, ref, cut):
        def there():
            if cut.start == 0:
                copies[at].wait()
            return ref[cut, :]

        return there

    tile = ua.shape[0] // 2
    pieces = vision_pieces(ua, ba, da)
    for first in (0, tile):
        cut = pl.ds(first, tile)
        pieces.append((far(0, ub_out, cut), functools.partial(lambda cut: bb[cut], cut), far(1, db_out, cut)))
    out_ref[...] = feed_forward(rows_ref[...], pieces).astype(BF16)
    token_ref[...] = jnp.zeros_like(token_ref)


def pass_quarter(place_ref, ref, out_ref, sems):
    quarter = out_ref.shape[0]
    first = pl.multiple_of((2 * place_ref[0] + place_ref[1]) * quarter, quarter)
    return start_copies([(ref.at[pl.ds(first, quarter)], out_ref)], sems)


def order_kernel(place_ref, mine_ref, other_ref, out_ref):
    quarter = mine_ref.shape[0]
    for chip in range(2):
        out_ref[pl.ds(chip * quarter, quarter), :] = jnp.where(place_ref[1] == chip, mine_ref[...], other_ref[...])


def pass_on(core_ref, ref, out_ref, sem):
    half = out_ref.shape[0]
    first = pl.multiple_of(core_ref[0] * half, half)
    return start_copies([(ref.at[pl.ds(first, half)], out_ref)], sem)


def pass_kernel(core_ref, side_ref, *refs):
    half_ref, sems = refs[-2:]
    for copy in pass_on(core_ref, side_ref, half_ref, sems):
        copy.wait()


def second_kernel(core_ref, rows_ref, ua, ba, da, ub, bb, db, before_ref, *refs):
    if len(refs) > 2:
        side_ref, embed_ref, _, half_ref, embed_out_ref, out_ref, token_ref, sems = refs
        copies = pass_quarter(core_ref, side_ref, half_ref, sems)
        embed_out_ref[...] = embed_ref[...]
    else:
        out_ref, token_ref = refs
        copies = ()
    total = feed_forward(rows_ref[...], vision_pieces(ua, ba, da) + vision_pieces(ub, bb, db))
    out_ref[...] = total.astype(BF16)
    token_ref[...] = jnp.zeros_like(token_ref)
    for copy in copies:
        copy.wait()


def own_kernel(first_ref, second_ref, ua, ba, da, ub, bb, db, before_ref, back_ref, proj, out_ref, proj_out, sems):
    copies = start_copies([(proj, proj_out)], sems)
    half = first_ref.shape[0]
    rows = jnp.concatenate([first_ref[...], second_ref[...]], axis=0)
    total = feed_forward(rows, vision_pieces(ua, ba, da) + vision_pieces(ub, bb, db))
    out_ref[pl.ds(0, half), :] = total[:half] + back_ref[...].astype(F32)
    out_ref[pl.ds(half, half), :] = total[half:]
    for copy in copies:
        copy.wait()


def merge_kernel(patches_ref, own_ref, back_ref, gain_ref, proj_ref, place_ref, where_ref, out_ref):
    rows, width = patches_ref.shape
    count = rows // 8
    wide = plane_rows(patches_ref[...])
    merged = None
    for plane in range(4):
        halves = []
        for half in range(2):
            here = 4 * count * half + plane * count
            vis_out = wide[here : here + count] + own_ref[pl.ds(here, count), :]
            if half:
                vis_out = vis_out + back_ref[pl.ds(plane * count, count), :].astype(F32)
            halves.append(normalize(vis_out, gain_ref[...]).astype(BF16))
        proj = proj_ref[pl.ds(plane * width, width), :]
        part = jnp.dot(jnp.concatenate(halves, axis=0), proj, preferred_element_type=F32)
        merged = part if merged is None else merged + part
    placed = jnp.dot(place_ref[...], merged.astype(BF16), preferred_element_type=F32)
    out_ref[:, :width] = placed.astype(BF16)
    out_ref[:, width:] = where_ref[...]


def place_text_rows(which, capacity, embed, got):
    width = embed.shape[1]
    where = got[:, width:].astype(F32)
    token = lax.broadcasted_iota(jnp.int32, where.shape, 1).astype(F32)
    side_of = lax.broadcasted_iota(jnp.int32, where.shape, 0) // capacity % 2
    pick = ((where == token) & (side_of == which)).astype(F32).astype(BF16)
    by_token = (((0,), (0,)), ((), ()))
    picked = lax.dot_general(pick, got[:, :width], by_token, preferred_element_type=F32)
    taken = lax.dot_general(pick, jnp.ones((pick.shape[0], 128), BF16), by_token, preferred_element_type=F32)
    return jnp.where(taken[:, :1] > 0.5, picked, embed.astype(F32))


def load_text(rows, slices, halves, rooms, up, down, sems):
    half = up.shape[1] // 2
    pairs = list(zip(rows, rooms))
    waits = []
    for at in range(len(slices) // 2):
        for ref, room in ((slices[2 * at], up), (slices[2 * at + 1], down)):
            waits.append([len(pairs)])
            pairs.append((ref, room.at[at]))
    for at, room in enumerate((up, down)):
        if halves:
            waits.append([len(pairs), len(pairs) + 1])
        for number, ref in enumerate(halves[2 * at : 2 * at + 2]):
            pairs.append((ref, room.at[3, pl.ds(number * half, half)]))
    copies = start_copies(pairs, sems)

    def read(at):
        for number in waits[at]:
            copies[number].wait()
        return (up, down)[at % 2][at // 2]

    pieces = [(functools.partial(read, at), None, functools.partial(read, at + 1)) for at in range(0, len(waits), 2)]
    for copy in copies[: len(rows)]:
        copy.wait()
    return pieces


def theirs_kernel(capacity, embed_ref, got_ref, *refs):
    slices, gain_ref, normed_ref, total_ref = refs[:4], refs[4], refs[5], refs[6]
    embed, got, up, down, sems = refs[7:]
    pieces = load_text((embed_ref, got_ref), slices, (), (embed, got), up, down, sems)
    text_rows = place_text_rows(1, capacity, embed[...], got[...])
    normed = normalize(text_rows, gain_ref[...]).astype(BF16)
    normed_ref[...] = normed
    total_ref[...] = feed_forward(normed, pieces)


def theirs_more_kernel(normed_ref, total_ref, up_ref, down_ref, out_ref, up, down, sems):
    pieces = load_text((), (up_ref, down_ref), (), (), up, down, sems)
    out_ref[...] = total_ref[...] + feed_forward(normed_ref[...], pieces)


def theirs_last_kernel(normed_ref, total_ref, up_ref, other_up_ref, down_ref, other_down_ref, out_ref):
    def both(mine_ref, other_ref):
        return lambda: jnp.concatenate([mine_ref[...], other_ref[...]], axis=0)

    total = feed_forward(normed_ref[...], [(both(up_ref, other_up_ref), None, both(down_ref, other_down_ref))])
    out_ref[...] = (total_ref[...] + total).astype(BF16)


def mine_kernel(capacity, embed_ref, got_ref, *refs):
    slices, halves, gain_ref, out_ref = refs[:6], refs[6:10], refs[10], refs[11]
    embed, got, up, down, sems = refs[12:]
    pieces = load_text((embed_ref, got_ref), slices, halves, (embed, got), up, down, sems)
    text_rows = place_text_rows(0, capacity, embed[...], got[...])
    out_ref[...] = text_rows + feed_forward(normalize(text_rows, gain_ref[...]).astype(BF16), pieces)


def per_device(
    patches,
    vis_gain,
    vis_up,
    vis_bias,
    vis_down,
    merge_gain,
    merge_proj,
    text_embed,
    slot_index,
    text_gain,
    text_up,
    text_down,
):
    cycle_size = lax.axis_size("blk")
    merged_count = slot_index.shape[0]
    token_count, width = text_embed.shape
    patch_count = patches.shape[0]
    capacity = 2 * merged_count // cycle_size
    paired = cycle_size == 8
    sides = 2 if paired else 1

    target = slot_index // token_count % cycle_size
    position = slot_index % token_count
    one_hot = (target[:, None] == jnp.arange(cycle_size, dtype=jnp.int32)[None, :]).astype(jnp.int32)
    rank = jnp.sum((jnp.cumsum(one_hot, axis=0) - one_hot) * one_hot, axis=1)
    sent = jnp.arange(cycle_size * sides * capacity, dtype=jnp.int32)[:, None]
    owner = sent // (sides * capacity) ^ (4 * (sent // capacity % sides))
    chosen = (target[None, :] == owner) & (rank[None, :] == sent % capacity)
    place = chosen.astype(BF16)
    where = jnp.max(jnp.where(chosen, position[None, :], -1), axis=1, keepdims=True)
    where = jnp.broadcast_to(where.astype(BF16), (where.shape[0], 128))

    core = (lax.axis_index("seq") % 2).reshape(1)
    core_and_x = jnp.stack([lax.axis_index("seq") % 2, lax.axis_index("seq") // 2 % 2])
    half_rows = jax.ShapeDtypeStruct((patch_count // 2, width), BF16)
    far_up, far_down = swap(vis_up, "seq", 1), swap(vis_down, "seq", 1)
    other_bias = swap(after(vis_bias, far_up), "seq", 1)
    first, second, normed = call(
        norm_patches_kernel, "norm_patches", (half_rows, half_rows, TOKEN), (patches, vis_gain), megabytes=40
    )
    far_first, far_second = swap(first, "seq", 2), swap(second, "seq", 2)
    near_up, near_down = call(
        bring_kernel,
        "bring_vision",
        (like(vis_up), like(vis_down)),
        (vis_up, vis_down, normed),
        stored=(0, 1),
        copies=2,
        megabytes=44,
    )
    args = (far_first, near_up, vis_bias, near_down, far_up, other_bias, far_down)
    outs = (half_rows, TOKEN, like(vis_up), like(vis_down))
    if paired:
        side_up, side_down = swap_by_core(text_up, (1, 2)), swap_by_core(text_down, (1, 2))
    part_first, first_done, far_up, far_down = call(
        first_kernel, "vision_first", outs, args, stored=(4, 6), copies=2, megabytes=38
    )
    weights = (near_up, vis_bias, near_down, far_up, other_bias, far_down)
    back_first = swap(part_first, "seq", 2)
    args = (core_and_x, far_second, *weights, first_done)
    outs = (half_rows, TOKEN)
    half_slice = jax.ShapeDtypeStruct((text_up.shape[0] // 2, width), BF16)
    quarter_slice = jax.ShapeDtypeStruct((text_up.shape[0] // 4, width), BF16)
    if paired:
        side_up, across_up, other_embed, part_second, second_done = call(
            second_kernel,
            "vision_second",
            (like(side_up), quarter_slice, like(text_embed), *outs),
            args + (side_up, text_embed),
            aliases={len(args): 0},
            copies=1,
            scalars=1,
            microseconds=30,
        )
        other_up, across_up = swap(side_up, "seq", 1), swap_by_core(across_up, (2, 1))
        other_embed = swap(other_embed, "blk", 4)
    else:
        part_second, second_done = call(second_kernel, "vision_second", outs, args, scalars=1, microseconds=30)
    back_second = swap(part_second, "seq", 2)
    own_rows = jax.ShapeDtypeStruct((patch_count, width), F32)
    own, merge_proj = call(
        own_kernel,
        "vision_own",
        (own_rows, like(merge_proj)),
        (first, second, *weights, second_done, back_first, merge_proj),
        stored=(10,),
        microseconds=10,
        copies=1,
    )
    sent_rows = jax.ShapeDtypeStruct((place.shape[0], width + 128), BF16)
    args = (patches, own, back_second, merge_gain, merge_proj, place, where)
    send = call(merge_kernel, "merge_rows", sent_rows, args)
    if paired:
        side_down, across_down = call(
            pass_kernel,
            "pass_down",
            (like(side_down), half_slice),
            (core, side_down, send),
            aliases={1: 0},
            scalars=1,
            stored=(2,),
            copies=1,
            microseconds=0.001,
        )
        other_embed, across_up = call(
            same_kernel,
            "gate",
            (like(other_embed), like(across_up)),
            (other_embed, across_up, send),
            aliases={0: 0, 1: 1},
            stored=(2,),
            microseconds=9,
        )
        across_up = call(
            order_kernel,
            "order_across",
            half_slice,
            (core_and_x, across_up, swap(across_up, "seq", 2)),
            scalars=1,
            microseconds=0.001,
        )
        other_down, across_down = swap(side_down, "seq", 1), swap_by_core(across_down, (2, 1))
    got = lax.all_to_all(send, "blk", split_axis=0, concat_axis=0, tiled=True)
    if paired:
        got = after(got, send, microseconds=6)
        slices = (text_up, text_down, side_up, side_down, other_up, other_down)
        room = (
            pltpu.VMEM(text_embed.shape, BF16),
            pltpu.VMEM(got.shape, BF16),
            pltpu.VMEM((4, *text_up.shape), BF16),
            pltpu.VMEM((4, *text_up.shape), BF16),
        )
        sums = jax.ShapeDtypeStruct((token_count, width), F32)
        text_normed, total = call(
            functools.partial(theirs_kernel, capacity),
            "text_theirs",
            (like(text_embed), sums),
            (other_embed, got, *slices[:4], text_gain),
            stored=tuple(range(6)),
            copies=6,
            scratch=(*room[:2], *(pltpu.VMEM((2, *text_up.shape), BF16) for _ in range(2))),
            megabytes=52,
        )
        total = call(
            theirs_more_kernel,
            "text_theirs_more",
            sums,
            (text_normed, total, *slices[4:]),
            stored=(2, 3),
            copies=2,
            scratch=tuple(pltpu.VMEM((1, *text_up.shape), BF16) for _ in range(2)),
        )
        across_down = after(across_down, text_normed)
        halves = (across_up, swap(across_up, "seq", 1), across_down, swap(across_down, "seq", 1))
        theirs = call(theirs_last_kernel, "text_theirs_last", like(text_embed), (text_normed, total, *halves))
        mine = call(
            functools.partial(mine_kernel, capacity),
            "text_mine",
            sums,
            (text_embed, got, *slices, *halves, text_gain),
            stored=tuple(range(12)),
            copies=12,
            scratch=room,
            megabytes=24,
        )
        return (mine + swap(theirs, "blk", 4).astype(F32)).astype(BF16)
    tokens = jnp.arange(token_count, dtype=jnp.int32).astype(BF16)
    pick = (got[:, width:][:, :1] == tokens[None, :]).astype(BF16)
    picked = lax.dot_general(pick, got[:, :width], (((0,), (0,)), ((), ())), preferred_element_type=F32)
    taken = jnp.sum(pick.astype(F32), axis=0)[:, None] > 0.5
    text_rows = jnp.where(taken, picked, text_embed.astype(F32))
    text_normed = normalize(text_rows, text_gain).astype(BF16)
    gathered_tokens = lax.all_gather(text_normed, "blk", axis=0, tiled=True)
    hidden = gelu(up_project(gathered_tokens, text_up)).astype(BF16)
    text_mlp = lax.psum_scatter(
        jnp.dot(hidden, text_down, preferred_element_type=F32).astype(BF16),
        "blk",
        scatter_dimension=0,
        tiled=True,
    ).astype(F32)
    return (text_rows + text_mlp).astype(BF16)


def solution(mesh):
    placed = (
        P(("seq", "blk"), None),
        P(),
        P("seq", None),
        P("seq"),
        P("seq", None),
        P(),
        P(),
        P(("seq", "blk"), None),
        P(("seq", "blk")),
        P(),
        P("blk", None),
        P("blk", None),
    )
    return jax.shard_map(
        per_device, mesh=mesh, in_specs=placed, out_specs=P(("seq", "blk"), None), check_vma=False
    )
```

```python
import functools

import jax
import jax.numpy as jnp
from jax import lax
from jax.experimental import pallas as pl
from jax.experimental.pallas import tpu as pltpu
from jax.sharding import PartitionSpec as P

F32 = jnp.float32
BF16 = jnp.bfloat16
VMEM = pl.BlockSpec(memory_space=pltpu.VMEM)
STORED = pl.BlockSpec(memory_space=pltpu.HBM)
SMEM = pl.BlockSpec(memory_space=pltpu.SMEM)
TOKEN = jax.ShapeDtypeStruct((8, 128), F32)


def like(x):
    return jax.ShapeDtypeStruct(x.shape, x.dtype)


def cost(microseconds):
    return pl.CostEstimate(flops=int(microseconds * 1e9), bytes_accessed=1000, transcendentals=0)


def call(kernel, name, out_shape, args, microseconds=0.001, aliases=None, scalars=0, stored=(), copies=0, scratch=(), megabytes=16):
    aliases = aliases or {}
    stored = (*stored, *aliases)
    specs = [SMEM] * scalars + [STORED if at in stored else VMEM for at in range(scalars, len(args))]
    single = not isinstance(out_shape, tuple)
    out_shape = (out_shape,) if single else out_shape
    outs = pl.pallas_call(
        kernel,
        out_shape=out_shape,
        in_specs=specs,
        out_specs=tuple(STORED if at in aliases.values() else VMEM for at in range(len(out_shape))),
        input_output_aliases=aliases,
        scratch_shapes=[*scratch, *([pltpu.SemaphoreType.DMA((copies,))] if copies else [])],
        compiler_params=pltpu.CompilerParams(vmem_limit_bytes=megabytes * 1024 * 1024),
        cost_estimate=cost(microseconds),
        name=name,
    )(*args)
    return outs[0] if single else outs


def normalize(values, row_gain):
    values = values.astype(F32)
    center = values - jnp.mean(values, axis=-1, keepdims=True)
    spread = jnp.mean(center * center, axis=-1, keepdims=True)
    return center * lax.rsqrt(spread + 1e-06) * row_gain


def gelu(v):
    half = 0.5 * v
    return half + half * jnp.tanh(v * (0.7978845608028654 + 0.035677408136300125 * (v * v)))


def up_project(rows_in, up_piece):
    return lax.dot_general(rows_in, up_piece, (((1,), (1,)), ((), ())), preferred_element_type=F32)


def swap(x, axis, bit):
    size = lax.axis_size(axis)
    return lax.ppermute(x, axis, [(i, i ^ bit) for i in range(size)])


def swap_by_core(x, bit_of_core):
    seq_size, blk_size = lax.axis_size("seq"), lax.axis_size("blk")
    pairs = [(s * blk_size + b, s * blk_size + (b ^ bit_of_core[s % 2])) for s in range(seq_size) for b in range(blk_size)]
    return lax.ppermute(x, ("seq", "blk"), pairs)


def plane_rows(patches):
    rows = patches.shape[0]
    count = rows // 8
    place = lax.broadcasted_iota(jnp.int32, (rows, rows), 0)
    source = lax.broadcasted_iota(jnp.int32, (rows, rows), 1)
    half, plane, window = place // (4 * count), place // count % 4, place % count
    order = (source == 4 * (count * half + window) + plane).astype(BF16)
    return jnp.dot(order, patches, preferred_element_type=F32)


def norm_patches_kernel(patches_ref, gain_ref, first_ref, second_ref, token_ref):
    rows = patches_ref.shape[0]
    normed = normalize(plane_rows(patches_ref[...]), gain_ref[...]).astype(BF16)
    first_ref[...] = normed[: rows // 2]
    second_ref[...] = normed[rows // 2 :]
    token_ref[...] = jnp.zeros_like(token_ref)


def start_copies(pairs, sems):
    copies = [pltpu.make_async_copy(source, goal, sems.at[at]) for at, (source, goal) in enumerate(pairs)]
    for copy in copies:
        copy.start()
    return copies


def same_kernel(*refs):
    pass


def after(x, before, microseconds=0.001):
    return call(same_kernel, "after", like(x), (x, before), microseconds=microseconds, aliases={0: 0}, stored=(1,))


def feed_forward(rows, pieces):
    def pre(piece):
        up, bias, _ = piece
        product = up_project(rows, up())
        return product if bias is None else product + bias()

    total, ready = None, pre(pieces[0])
    for at, (_, _, down) in enumerate(pieces):
        later = pre(pieces[at + 1]) if at + 1 < len(pieces) else None
        part = jnp.dot(gelu(ready).astype(BF16), down(), preferred_element_type=F32)
        total = part if total is None else total + part
        ready = later
    return total


def vision_pieces(up, bias, down):
    pieces = []
    tile = up.shape[0] // 2
    for at in (0, tile):
        cut = pl.ds(at, tile)
        pieces.append(
            (
                functools.partial(lambda ref, cut: ref[cut, :], up, cut),
                functools.partial(lambda ref, cut: ref[cut], bias, cut),
                functools.partial(lambda ref, cut: ref[cut, :], down, cut),
            )
        )
    return pieces


def bring_kernel(ua, da, before_ref, ua_out, da_out, sems):
    for copy in start_copies([(ua, ua_out), (da, da_out)], sems):
        copy.wait()


def first_kernel(rows_ref, ua, ba, da, ub, bb, db, out_ref, token_ref, ub_out, db_out, sems):
    copies = start_copies([(ub, ub_out), (db, db_out)], sems)

    def far(at, ref, cut):
        def there():
            if cut.start == 0:
                copies[at].wait()
            return ref[cut, :]

        return there

    tile = ua.shape[0] // 2
    pieces = vision_pieces(ua, ba, da)
    for first in (0, tile):
        cut = pl.ds(first, tile)
        pieces.append((far(0, ub_out, cut), functools.partial(lambda cut: bb[cut], cut), far(1, db_out, cut)))
    out_ref[...] = feed_forward(rows_ref[...], pieces).astype(BF16)
    token_ref[...] = jnp.zeros_like(token_ref)


def pass_quarter(place_ref, ref, out_ref, sems):
    quarter = out_ref.shape[0]
    first = pl.multiple_of((2 * place_ref[0] + place_ref[1]) * quarter, quarter)
    return start_copies([(ref.at[pl.ds(first, quarter)], out_ref)], sems)


def order_kernel(place_ref, mine_ref, other_ref, out_ref):
    quarter = mine_ref.shape[0]
    for chip in range(2):
        out_ref[pl.ds(chip * quarter, quarter), :] = jnp.where(place_ref[1] == chip, mine_ref[...], other_ref[...])


def pass_on(core_ref, ref, out_ref, sem):
    half = out_ref.shape[0]
    first = pl.multiple_of(core_ref[0] * half, half)
    return start_copies([(ref.at[pl.ds(first, half)], out_ref)], sem)


def pass_kernel(core_ref, side_ref, *refs):
    half_ref, sems = refs[-2:]
    for copy in pass_on(core_ref, side_ref, half_ref, sems):
        copy.wait()


def second_kernel(core_ref, rows_ref, ua, ba, da, ub, bb, db, before_ref, *refs):
    if len(refs) > 2:
        side_ref, embed_ref, _, half_ref, embed_out_ref, out_ref, token_ref, sems = refs
        copies = pass_quarter(core_ref, side_ref, half_ref, sems)
        embed_out_ref[...] = embed_ref[...]
    else:
        out_ref, token_ref = refs
        copies = ()
    total = feed_forward(rows_ref[...], vision_pieces(ua, ba, da) + vision_pieces(ub, bb, db))
    out_ref[...] = total.astype(BF16)
    token_ref[...] = jnp.zeros_like(token_ref)
    for copy in copies:
        copy.wait()


def own_kernel(first_ref, second_ref, ua, ba, da, ub, bb, db, before_ref, back_ref, proj, out_ref, proj_out, sems):
    copies = start_copies([(proj, proj_out)], sems)
    half = first_ref.shape[0]
    rows = jnp.concatenate([first_ref[...], second_ref[...]], axis=0)
    total = feed_forward(rows, vision_pieces(ua, ba, da) + vision_pieces(ub, bb, db))
    out_ref[pl.ds(0, half), :] = total[:half] + back_ref[...].astype(F32)
    out_ref[pl.ds(half, half), :] = total[half:]
    for copy in copies:
        copy.wait()


def merge_kernel(patches_ref, own_ref, back_ref, gain_ref, proj_ref, place_ref, where_ref, out_ref):
    rows, width = patches_ref.shape
    count = rows // 8
    wide = plane_rows(patches_ref[...])
    merged = None
    for plane in range(4):
        halves = []
        for half in range(2):
            here = 4 * count * half + plane * count
            vis_out = wide[here : here + count] + own_ref[pl.ds(here, count), :]
            if half:
                vis_out = vis_out + back_ref[pl.ds(plane * count, count), :].astype(F32)
            halves.append(normalize(vis_out, gain_ref[...]).astype(BF16))
        proj = proj_ref[pl.ds(plane * width, width), :]
        part = jnp.dot(jnp.concatenate(halves, axis=0), proj, preferred_element_type=F32)
        merged = part if merged is None else merged + part
    placed = jnp.dot(place_ref[...], merged.astype(BF16), preferred_element_type=F32)
    out_ref[:, :width] = placed.astype(BF16)
    out_ref[:, width:] = where_ref[...]


def place_text_rows(which, capacity, embed, got):
    width = embed.shape[1]
    where = got[:, width:].astype(F32)
    token = lax.broadcasted_iota(jnp.int32, where.shape, 1).astype(F32)
    side_of = lax.broadcasted_iota(jnp.int32, where.shape, 0) // capacity % 2
    pick = ((where == token) & (side_of == which)).astype(F32).astype(BF16)
    by_token = (((0,), (0,)), ((), ()))
    picked = lax.dot_general(pick, got[:, :width], by_token, preferred_element_type=F32)
    taken = lax.dot_general(pick, jnp.ones((pick.shape[0], 128), BF16), by_token, preferred_element_type=F32)
    return jnp.where(taken[:, :1] > 0.5, picked, embed.astype(F32))


def load_text(rows, slices, halves, rooms, up, down, sems):
    half = up.shape[1] // 2
    pairs = list(zip(rows, rooms))
    waits = []
    for at in range(len(slices) // 2):
        for ref, room in ((slices[2 * at], up), (slices[2 * at + 1], down)):
            waits.append([len(pairs)])
            pairs.append((ref, room.at[at]))
    for at, room in enumerate((up, down)):
        if halves:
            waits.append([len(pairs), len(pairs) + 1])
        for number, ref in enumerate(halves[2 * at : 2 * at + 2]):
            pairs.append((ref, room.at[3, pl.ds(number * half, half)]))
    copies = start_copies(pairs, sems)

    def read(at):
        for number in waits[at]:
            copies[number].wait()
        return (up, down)[at % 2][at // 2]

    pieces = [(functools.partial(read, at), None, functools.partial(read, at + 1)) for at in range(0, len(waits), 2)]
    for copy in copies[: len(rows)]:
        copy.wait()
    return pieces


def theirs_kernel(capacity, embed_ref, got_ref, *refs):
    slices, gain_ref, normed_ref, total_ref = refs[:4], refs[4], refs[5], refs[6]
    embed, got, up, down, sems = refs[7:]
    pieces = load_text((embed_ref, got_ref), slices, (), (embed, got), up, down, sems)
    text_rows = place_text_rows(1, capacity, embed[...], got[...])
    normed = normalize(text_rows, gain_ref[...]).astype(BF16)
    normed_ref[...] = normed
    total_ref[...] = feed_forward(normed, pieces)


def theirs_more_kernel(normed_ref, total_ref, up_ref, down_ref, out_ref, up, down, sems):
    pieces = load_text((), (up_ref, down_ref), (), (), up, down, sems)
    out_ref[...] = total_ref[...] + feed_forward(normed_ref[...], pieces)


def theirs_last_kernel(normed_ref, total_ref, up_ref, other_up_ref, down_ref, other_down_ref, out_ref):
    def both(mine_ref, other_ref):
        return lambda: jnp.concatenate([mine_ref[...], other_ref[...]], axis=0)

    total = feed_forward(normed_ref[...], [(both(up_ref, other_up_ref), None, both(down_ref, other_down_ref))])
    out_ref[...] = (total_ref[...] + total).astype(BF16)


def mine_kernel(capacity, embed_ref, got_ref, *refs):
    slices, halves, gain_ref, out_ref = refs[:6], refs[6:10], refs[10], refs[11]
    embed, got, up, down, sems = refs[12:]
    pieces = load_text((embed_ref, got_ref), slices, halves, (embed, got), up, down, sems)
    text_rows = place_text_rows(0, capacity, embed[...], got[...])
    out_ref[...] = text_rows + feed_forward(normalize(text_rows, gain_ref[...]).astype(BF16), pieces)


def per_device(
    patches,
    vis_gain,
    vis_up,
    vis_bias,
    vis_down,
    merge_gain,
    merge_proj,
    text_embed,
    slot_index,
    text_gain,
    text_up,
    text_down,
):
    cycle_size = lax.axis_size("blk")
    merged_count = slot_index.shape[0]
    token_count, width = text_embed.shape
    patch_count = patches.shape[0]
    capacity = 2 * merged_count // cycle_size
    paired = cycle_size == 8
    sides = 2 if paired else 1

    target = slot_index // token_count % cycle_size
    position = slot_index % token_count
    one_hot = (target[:, None] == jnp.arange(cycle_size, dtype=jnp.int32)[None, :]).astype(jnp.int32)
    rank = jnp.sum((jnp.cumsum(one_hot, axis=0) - one_hot) * one_hot, axis=1)
    sent = jnp.arange(cycle_size * sides * capacity, dtype=jnp.int32)[:, None]
    owner = sent // (sides * capacity) ^ (4 * (sent // capacity % sides))
    chosen = (target[None, :] == owner) & (rank[None, :] == sent % capacity)
    place = chosen.astype(BF16)
    where = jnp.max(jnp.where(chosen, position[None, :], -1), axis=1, keepdims=True)
    where = jnp.broadcast_to(where.astype(BF16), (where.shape[0], 128))

    core = (lax.axis_index("seq") % 2).reshape(1)
    core_and_x = jnp.stack([lax.axis_index("seq") % 2, lax.axis_index("seq") // 2 % 2])
    half_rows = jax.ShapeDtypeStruct((patch_count // 2, width), BF16)
    far_up, far_down = swap(vis_up, "seq", 1), swap(vis_down, "seq", 1)
    other_bias = swap(after(vis_bias, far_up), "seq", 1)
    first, second, normed = call(
        norm_patches_kernel, "norm_patches", (half_rows, half_rows, TOKEN), (patches, vis_gain), megabytes=60
    )
    far_first, far_second = swap(first, "seq", 2), swap(second, "seq", 2)
    near_up, near_down = call(
        bring_kernel,
        "bring_vision",
        (like(vis_up), like(vis_down)),
        (vis_up, vis_down, normed),
        stored=(0, 1),
        copies=2,
        megabytes=44,
    )
    args = (far_first, near_up, vis_bias, near_down, far_up, other_bias, far_down)
    outs = (half_rows, TOKEN, like(vis_up), like(vis_down))
    if paired:
        side_up, side_down = swap_by_core(text_up, (1, 2)), swap_by_core(text_down, (1, 2))
    part_first, first_done, far_up, far_down = call(
        first_kernel, "vision_first", outs, args, stored=(4, 6), copies=2, megabytes=38
    )
    weights = (near_up, vis_bias, near_down, far_up, other_bias, far_down)
    back_first = swap(part_first, "seq", 2)
    args = (core_and_x, far_second, *weights, first_done)
    outs = (half_rows, TOKEN)
    half_slice = jax.ShapeDtypeStruct((text_up.shape[0] // 2, width), BF16)
    quarter_slice = jax.ShapeDtypeStruct((text_up.shape[0] // 4, width), BF16)
    if paired:
        side_up, across_up, other_embed, part_second, second_done = call(
            second_kernel,
            "vision_second",
            (like(side_up), quarter_slice, like(text_embed), *outs),
            args + (side_up, text_embed),
            aliases={len(args): 0},
            copies=1,
            scalars=1,
            microseconds=30,
        )
        other_up, across_up = swap(side_up, "seq", 1), swap_by_core(across_up, (2, 1))
        other_embed = swap(other_embed, "blk", 4)
    else:
        part_second, second_done = call(second_kernel, "vision_second", outs, args, scalars=1, microseconds=30)
    back_second = swap(part_second, "seq", 2)
    own_rows = jax.ShapeDtypeStruct((patch_count, width), F32)
    own, merge_proj = call(
        own_kernel,
        "vision_own",
        (own_rows, like(merge_proj)),
        (first, second, *weights, second_done, back_first, merge_proj),
        stored=(10,),
        microseconds=10,
        copies=1,
    )
    sent_rows = jax.ShapeDtypeStruct((place.shape[0], width + 128), BF16)
    args = (patches, own, back_second, merge_gain, merge_proj, place, where)
    send = call(merge_kernel, "merge_rows", sent_rows, args)
    if paired:
        side_down, across_down = call(
            pass_kernel,
            "pass_down",
            (like(side_down), half_slice),
            (core, side_down, send),
            aliases={1: 0},
            scalars=1,
            stored=(2,),
            copies=1,
            microseconds=0.001,
        )
        other_embed, across_up = call(
            same_kernel,
            "gate",
            (like(other_embed), like(across_up)),
            (other_embed, across_up, send),
            aliases={0: 0, 1: 1},
            stored=(2,),
            microseconds=9,
        )
        across_up = call(
            order_kernel,
            "order_across",
            half_slice,
            (core_and_x, across_up, swap(across_up, "seq", 2)),
            scalars=1,
            microseconds=0.001,
        )
        other_down, across_down = swap(side_down, "seq", 1), swap_by_core(across_down, (2, 1))
    got = lax.all_to_all(send, "blk", split_axis=0, concat_axis=0, tiled=True)
    if paired:
        got = after(got, send, microseconds=6)
        slices = (text_up, text_down, side_up, side_down, other_up, other_down)
        room = (
            pltpu.VMEM(text_embed.shape, BF16),
            pltpu.VMEM(got.shape, BF16),
            pltpu.VMEM((4, *text_up.shape), BF16),
            pltpu.VMEM((4, *text_up.shape), BF16),
        )
        sums = jax.ShapeDtypeStruct((token_count, width), F32)
        text_normed, total = call(
            functools.partial(theirs_kernel, capacity),
            "text_theirs",
            (like(text_embed), sums),
            (other_embed, got, *slices[:4], text_gain),
            stored=tuple(range(6)),
            copies=6,
            scratch=(*room[:2], *(pltpu.VMEM((2, *text_up.shape), BF16) for _ in range(2))),
            megabytes=52,
        )
        total = call(
            theirs_more_kernel,
            "text_theirs_more",
            sums,
            (text_normed, total, *slices[4:]),
            stored=(2, 3),
            copies=2,
            scratch=tuple(pltpu.VMEM((1, *text_up.shape), BF16) for _ in range(2)),
        )
        across_down = after(across_down, text_normed)
        halves = (across_up, swap(across_up, "seq", 1), across_down, swap(across_down, "seq", 1))
        theirs = call(theirs_last_kernel, "text_theirs_last", like(text_embed), (text_normed, total, *halves))
        mine = call(
            functools.partial(mine_kernel, capacity),
            "text_mine",
            sums,
            (text_embed, got, *slices, *halves, text_gain),
            stored=tuple(range(12)),
            copies=12,
            scratch=room,
            megabytes=24,
        )
        return (mine + swap(theirs, "blk", 4).astype(F32)).astype(BF16)
    tokens = jnp.arange(token_count, dtype=jnp.int32).astype(BF16)
    pick = (got[:, width:][:, :1] == tokens[None, :]).astype(BF16)
    picked = lax.dot_general(pick, got[:, :width], (((0,), (0,)), ((), ())), preferred_element_type=F32)
    taken = jnp.sum(pick.astype(F32), axis=0)[:, None] > 0.5
    text_rows = jnp.where(taken, picked, text_embed.astype(F32))
    text_normed = normalize(text_rows, text_gain).astype(BF16)
    gathered_tokens = lax.all_gather(text_normed, "blk", axis=0, tiled=True)
    hidden = gelu(up_project(gathered_tokens, text_up)).astype(BF16)
    text_mlp = lax.psum_scatter(
        jnp.dot(hidden, text_down, preferred_element_type=F32).astype(BF16),
        "blk",
        scatter_dimension=0,
        tiled=True,
    ).astype(F32)
    return (text_rows + text_mlp).astype(BF16)


def solution(mesh):
    placed = (
        P(("seq", "blk"), None),
        P(),
        P("seq", None),
        P("seq"),
        P("seq", None),
        P(),
        P(),
        P(("seq", "blk"), None),
        P(("seq", "blk")),
        P(),
        P("blk", None),
        P("blk", None),
    )
    return jax.shard_map(
        per_device, mesh=mesh, in_specs=placed, out_specs=P(("seq", "blk"), None), check_vma=False
    )
```

```python
import functools

import jax
import jax.numpy as jnp
from jax import lax
from jax.experimental import pallas as pl
from jax.experimental.pallas import tpu as pltpu
from jax.sharding import PartitionSpec as P

F32 = jnp.float32
BF16 = jnp.bfloat16
VMEM = pl.BlockSpec(memory_space=pltpu.VMEM)
STORED = pl.BlockSpec(memory_space=pltpu.HBM)
SMEM = pl.BlockSpec(memory_space=pltpu.SMEM)
TOKEN = jax.ShapeDtypeStruct((8, 128), F32)


def like(x):
    return jax.ShapeDtypeStruct(x.shape, x.dtype)


def cost(microseconds):
    return pl.CostEstimate(flops=int(microseconds * 1e9), bytes_accessed=1000, transcendentals=0)


def call(kernel, name, out_shape, args, microseconds=0.001, aliases=None, scalars=0, stored=(), copies=0, scratch=(), megabytes=16):
    aliases = aliases or {}
    stored = (*stored, *aliases)
    specs = [SMEM] * scalars + [STORED if at in stored else VMEM for at in range(scalars, len(args))]
    single = not isinstance(out_shape, tuple)
    out_shape = (out_shape,) if single else out_shape
    outs = pl.pallas_call(
        kernel,
        out_shape=out_shape,
        in_specs=specs,
        out_specs=tuple(STORED if at in aliases.values() else VMEM for at in range(len(out_shape))),
        input_output_aliases=aliases,
        scratch_shapes=[*scratch, *([pltpu.SemaphoreType.DMA((copies,))] if copies else [])],
        compiler_params=pltpu.CompilerParams(vmem_limit_bytes=megabytes * 1024 * 1024),
        cost_estimate=cost(microseconds),
        name=name,
    )(*args)
    return outs[0] if single else outs


def normalize(values, row_gain):
    values = values.astype(F32)
    center = values - jnp.mean(values, axis=-1, keepdims=True)
    spread = jnp.mean(center * center, axis=-1, keepdims=True)
    return center * lax.rsqrt(spread + 1e-06) * row_gain


def gelu(v):
    half = 0.5 * v
    return half + half * jnp.tanh(v * (0.7978845608028654 + 0.035677408136300125 * (v * v)))


def up_project(rows_in, up_piece):
    return lax.dot_general(rows_in, up_piece, (((1,), (1,)), ((), ())), preferred_element_type=F32)


def swap(x, axis, bit):
    size = lax.axis_size(axis)
    return lax.ppermute(x, axis, [(i, i ^ bit) for i in range(size)])


def swap_by_core(x, bit_of_core):
    seq_size, blk_size = lax.axis_size("seq"), lax.axis_size("blk")
    pairs = [(s * blk_size + b, s * blk_size + (b ^ bit_of_core[s % 2])) for s in range(seq_size) for b in range(blk_size)]
    return lax.ppermute(x, ("seq", "blk"), pairs)


def plane_rows(patches):
    rows = patches.shape[0]
    count = rows // 8
    place = lax.broadcasted_iota(jnp.int32, (rows, rows), 0)
    source = lax.broadcasted_iota(jnp.int32, (rows, rows), 1)
    half, plane, window = place // (4 * count), place // count % 4, place % count
    order = (source == 4 * (count * half + window) + plane).astype(BF16)
    return jnp.dot(order, patches, preferred_element_type=F32)


def norm_patches_kernel(patches_ref, gain_ref, first_ref, second_ref, token_ref):
    rows = patches_ref.shape[0]
    normed = normalize(plane_rows(patches_ref[...]), gain_ref[...]).astype(BF16)
    first_ref[...] = normed[: rows // 2]
    second_ref[...] = normed[rows // 2 :]
    token_ref[...] = jnp.zeros_like(token_ref)


def start_copies(pairs, sems):
    copies = [pltpu.make_async_copy(source, goal, sems.at[at]) for at, (source, goal) in enumerate(pairs)]
    for copy in copies:
        copy.start()
    return copies


def same_kernel(*refs):
    pass


def after(x, before, microseconds=0.001):
    return call(same_kernel, "after", like(x), (x, before), microseconds=microseconds, aliases={0: 0}, stored=(1,))


def feed_forward(rows, pieces):
    def pre(piece):
        up, bias, _ = piece
        product = up_project(rows, up())
        return product if bias is None else product + bias()

    total, ready = None, pre(pieces[0])
    for at, (_, _, down) in enumerate(pieces):
        later = pre(pieces[at + 1]) if at + 1 < len(pieces) else None
        part = jnp.dot(gelu(ready).astype(BF16), down(), preferred_element_type=F32)
        total = part if total is None else total + part
        ready = later
    return total


def vision_pieces(up, bias, down):
    pieces = []
    tile = up.shape[0] // 2
    for at in (0, tile):
        cut = pl.ds(at, tile)
        pieces.append(
            (
                functools.partial(lambda ref, cut: ref[cut, :], up, cut),
                functools.partial(lambda ref, cut: ref[cut], bias, cut),
                functools.partial(lambda ref, cut: ref[cut, :], down, cut),
            )
        )
    return pieces


def bring_kernel(ua, da, before_ref, ua_out, da_out, sems):
    for copy in start_copies([(ua, ua_out), (da, da_out)], sems):
        copy.wait()


def first_kernel(rows_ref, ua, ba, da, ub, bb, db, out_ref, token_ref, ub_out, db_out, sems):
    copies = start_copies([(ub, ub_out), (db, db_out)], sems)

    def far(at, ref, cut):
        def there():
            if cut.start == 0:
                copies[at].wait()
            return ref[cut, :]

        return there

    tile = ua.shape[0] // 2
    pieces = vision_pieces(ua, ba, da)
    for first in (0, tile):
        cut = pl.ds(first, tile)
        pieces.append((far(0, ub_out, cut), functools.partial(lambda cut: bb[cut], cut), far(1, db_out, cut)))
    out_ref[...] = feed_forward(rows_ref[...], pieces).astype(BF16)
    token_ref[...] = jnp.zeros_like(token_ref)


def pass_quarter(place_ref, ref, out_ref, sems):
    quarter = out_ref.shape[0]
    first = pl.multiple_of((2 * place_ref[0] + place_ref[1]) * quarter, quarter)
    return start_copies([(ref.at[pl.ds(first, quarter)], out_ref)], sems)


def order_kernel(place_ref, mine_ref, other_ref, out_ref):
    quarter = mine_ref.shape[0]
    for chip in range(2):
        out_ref[pl.ds(chip * quarter, quarter), :] = jnp.where(place_ref[1] == chip, mine_ref[...], other_ref[...])


def pass_on(core_ref, ref, out_ref, sem):
    half = out_ref.shape[0]
    first = pl.multiple_of(core_ref[0] * half, half)
    return start_copies([(ref.at[pl.ds(first, half)], out_ref)], sem)


def pass_kernel(core_ref, side_ref, *refs):
    half_ref, sems = refs[-2:]
    for copy in pass_on(core_ref, side_ref, half_ref, sems):
        copy.wait()


def second_kernel(core_ref, rows_ref, ua, ba, da, ub, bb, db, before_ref, *refs):
    if len(refs) > 2:
        side_ref, embed_ref, _, half_ref, embed_out_ref, out_ref, token_ref, sems = refs
        copies = pass_quarter(core_ref, side_ref, half_ref, sems)
        embed_out_ref[...] = embed_ref[...]
    else:
        out_ref, token_ref = refs
        copies = ()
    total = feed_forward(rows_ref[...], vision_pieces(ua, ba, da) + vision_pieces(ub, bb, db))
    out_ref[...] = total.astype(BF16)
    token_ref[...] = jnp.zeros_like(token_ref)
    for copy in copies:
        copy.wait()


def own_kernel(first_ref, second_ref, ua, ba, da, ub, bb, db, before_ref, back_ref, proj, out_ref, proj_out, sems):
    copies = start_copies([(proj, proj_out)], sems)
    half = first_ref.shape[0]
    rows = jnp.concatenate([first_ref[...], second_ref[...]], axis=0)
    total = feed_forward(rows, vision_pieces(ua, ba, da) + vision_pieces(ub, bb, db))
    out_ref[pl.ds(0, half), :] = total[:half] + back_ref[...].astype(F32)
    out_ref[pl.ds(half, half), :] = total[half:]
    for copy in copies:
        copy.wait()


def merge_kernel(patches_ref, own_ref, back_ref, gain_ref, proj_ref, place_ref, where_ref, out_ref):
    rows, width = patches_ref.shape
    count = rows // 8
    wide = plane_rows(patches_ref[...])
    merged = None
    for plane in range(4):
        halves = []
        for half in range(2):
            here = 4 * count * half + plane * count
            vis_out = wide[here : here + count] + own_ref[pl.ds(here, count), :]
            if half:
                vis_out = vis_out + back_ref[pl.ds(plane * count, count), :].astype(F32)
            halves.append(normalize(vis_out, gain_ref[...]).astype(BF16))
        proj = proj_ref[pl.ds(plane * width, width), :]
        part = jnp.dot(jnp.concatenate(halves, axis=0), proj, preferred_element_type=F32)
        merged = part if merged is None else merged + part
    placed = jnp.dot(place_ref[...], merged.astype(BF16), preferred_element_type=F32)
    out_ref[:, :width] = placed.astype(BF16)
    out_ref[:, width:] = where_ref[...]


def place_text_rows(which, capacity, embed, got):
    width = embed.shape[1]
    where = got[:, width:].astype(F32)
    token = lax.broadcasted_iota(jnp.int32, where.shape, 1).astype(F32)
    side_of = lax.broadcasted_iota(jnp.int32, where.shape, 0) // capacity % 2
    pick = ((where == token) & (side_of == which)).astype(F32).astype(BF16)
    by_token = (((0,), (0,)), ((), ()))
    picked = lax.dot_general(pick, got[:, :width], by_token, preferred_element_type=F32)
    taken = lax.dot_general(pick, jnp.ones((pick.shape[0], 128), BF16), by_token, preferred_element_type=F32)
    return jnp.where(taken[:, :1] > 0.5, picked, embed.astype(F32))


def load_text(rows, slices, halves, rooms, up, down, sems):
    half = up.shape[1] // 2
    pairs = list(zip(rows, rooms))
    waits = []
    for at in range(len(slices) // 2):
        for ref, room in ((slices[2 * at], up), (slices[2 * at + 1], down)):
            waits.append([len(pairs)])
            pairs.append((ref, room.at[at]))
    for at, room in enumerate((up, down)):
        if halves:
            waits.append([len(pairs), len(pairs) + 1])
        for number, ref in enumerate(halves[2 * at : 2 * at + 2]):
            pairs.append((ref, room.at[3, pl.ds(number * half, half)]))
    copies = start_copies(pairs, sems)

    def read(at):
        for number in waits[at]:
            copies[number].wait()
        return (up, down)[at % 2][at // 2]

    pieces = [(functools.partial(read, at), None, functools.partial(read, at + 1)) for at in range(0, len(waits), 2)]
    for copy in copies[: len(rows)]:
        copy.wait()
    return pieces


def theirs_kernel(capacity, embed_ref, got_ref, *refs):
    slices, gain_ref, normed_ref, total_ref = refs[:4], refs[4], refs[5], refs[6]
    embed, got, up, down, sems = refs[7:]
    pieces = load_text((embed_ref, got_ref), slices, (), (embed, got), up, down, sems)
    text_rows = place_text_rows(1, capacity, embed[...], got[...])
    normed = normalize(text_rows, gain_ref[...]).astype(BF16)
    normed_ref[...] = normed
    total_ref[...] = feed_forward(normed, pieces)


def theirs_more_kernel(normed_ref, total_ref, up_ref, down_ref, out_ref, up, down, sems):
    pieces = load_text((), (up_ref, down_ref), (), (), up, down, sems)
    out_ref[...] = total_ref[...] + feed_forward(normed_ref[...], pieces)


def theirs_last_kernel(normed_ref, total_ref, *refs):
    halves, out_ref, (up, down, sems) = refs[:4], refs[4], refs[5:]
    half = up.shape[1] // 2
    pairs = [
        (ref, (up, down)[at // 2].at[0, pl.ds(at % 2 * half, half)]) for at, ref in enumerate(halves)
    ]
    copies = start_copies(pairs, sems)

    def both(at):
        def read():
            for copy in copies[at : at + 2]:
                copy.wait()
            return (up, down)[at // 2][0]

        return read

    total = feed_forward(normed_ref[...], [(both(0), None, both(2))])
    out_ref[...] = (total_ref[...] + total).astype(BF16)


def mine_kernel(capacity, embed_ref, got_ref, *refs):
    slices, halves, gain_ref, out_ref = refs[:6], refs[6:10], refs[10], refs[11]
    embed, got, up, down, sems = refs[12:]
    pieces = load_text((embed_ref, got_ref), slices, halves, (embed, got), up, down, sems)
    text_rows = place_text_rows(0, capacity, embed[...], got[...])
    out_ref[...] = text_rows + feed_forward(normalize(text_rows, gain_ref[...]).astype(BF16), pieces)


def per_device(
    patches,
    vis_gain,
    vis_up,
    vis_bias,
    vis_down,
    merge_gain,
    merge_proj,
    text_embed,
    slot_index,
    text_gain,
    text_up,
    text_down,
):
    cycle_size = lax.axis_size("blk")
    merged_count = slot_index.shape[0]
    token_count, width = text_embed.shape
    patch_count = patches.shape[0]
    capacity = 2 * merged_count // cycle_size
    paired = cycle_size == 8
    sides = 2 if paired else 1

    target = slot_index // token_count % cycle_size
    position = slot_index % token_count
    one_hot = (target[:, None] == jnp.arange(cycle_size, dtype=jnp.int32)[None, :]).astype(jnp.int32)
    rank = jnp.sum((jnp.cumsum(one_hot, axis=0) - one_hot) * one_hot, axis=1)
    sent = jnp.arange(cycle_size * sides * capacity, dtype=jnp.int32)[:, None]
    owner = sent // (sides * capacity) ^ (4 * (sent // capacity % sides))
    chosen = (target[None, :] == owner) & (rank[None, :] == sent % capacity)
    place = chosen.astype(BF16)
    where = jnp.max(jnp.where(chosen, position[None, :], -1), axis=1, keepdims=True)
    where = jnp.broadcast_to(where.astype(BF16), (where.shape[0], 128))

    core = (lax.axis_index("seq") % 2).reshape(1)
    core_and_x = jnp.stack([lax.axis_index("seq") % 2, lax.axis_index("seq") // 2 % 2])
    half_rows = jax.ShapeDtypeStruct((patch_count // 2, width), BF16)
    far_up, far_down = swap(vis_up, "seq", 1), swap(vis_down, "seq", 1)
    other_bias = swap(after(vis_bias, far_up), "seq", 1)
    first, second, normed = call(
        norm_patches_kernel, "norm_patches", (half_rows, half_rows, TOKEN), (patches, vis_gain), megabytes=60
    )
    far_first, far_second = swap(first, "seq", 2), swap(second, "seq", 2)
    near_up, near_down = call(
        bring_kernel,
        "bring_vision",
        (like(vis_up), like(vis_down)),
        (vis_up, vis_down, normed),
        stored=(0, 1),
        copies=2,
        megabytes=44,
    )
    args = (far_first, near_up, vis_bias, near_down, far_up, other_bias, far_down)
    outs = (half_rows, TOKEN, like(vis_up), like(vis_down))
    if paired:
        side_up, side_down = swap_by_core(text_up, (1, 2)), swap_by_core(text_down, (1, 2))
    part_first, first_done, far_up, far_down = call(
        first_kernel, "vision_first", outs, args, stored=(4, 6), copies=2, megabytes=38
    )
    weights = (near_up, vis_bias, near_down, far_up, other_bias, far_down)
    back_first = swap(part_first, "seq", 2)
    args = (core_and_x, far_second, *weights, first_done)
    outs = (half_rows, TOKEN)
    half_slice = jax.ShapeDtypeStruct((text_up.shape[0] // 2, width), BF16)
    quarter_slice = jax.ShapeDtypeStruct((text_up.shape[0] // 4, width), BF16)
    if paired:
        side_up, across_up, other_embed, part_second, second_done = call(
            second_kernel,
            "vision_second",
            (like(side_up), quarter_slice, like(text_embed), *outs),
            args + (side_up, text_embed),
            aliases={len(args): 0},
            copies=1,
            scalars=1,
            microseconds=30,
        )
        other_up, across_up = swap(side_up, "seq", 1), swap_by_core(across_up, (2, 1))
        other_embed = swap(other_embed, "blk", 4)
    else:
        part_second, second_done = call(second_kernel, "vision_second", outs, args, scalars=1, microseconds=30)
    back_second = swap(part_second, "seq", 2)
    own_rows = jax.ShapeDtypeStruct((patch_count, width), F32)
    own, merge_proj = call(
        own_kernel,
        "vision_own",
        (own_rows, like(merge_proj)),
        (first, second, *weights, second_done, back_first, merge_proj),
        stored=(10,),
        microseconds=10,
        copies=1,
    )
    sent_rows = jax.ShapeDtypeStruct((place.shape[0], width + 128), BF16)
    args = (patches, own, back_second, merge_gain, merge_proj, place, where)
    send = call(merge_kernel, "merge_rows", sent_rows, args)
    if paired:
        side_down, across_down = call(
            pass_kernel,
            "pass_down",
            (like(side_down), half_slice),
            (core, side_down, send),
            aliases={1: 0},
            scalars=1,
            stored=(2,),
            copies=1,
            microseconds=0.001,
        )
        other_embed, across_up = call(
            same_kernel,
            "gate",
            (like(other_embed), like(across_up)),
            (other_embed, across_up, send),
            aliases={0: 0, 1: 1},
            stored=(2,),
            microseconds=9,
        )
        across_up = call(
            order_kernel,
            "order_across",
            half_slice,
            (core_and_x, across_up, swap(across_up, "seq", 2)),
            scalars=1,
            microseconds=0.001,
        )
        other_down, across_down = swap(side_down, "seq", 1), swap_by_core(across_down, (2, 1))
    got = lax.all_to_all(send, "blk", split_axis=0, concat_axis=0, tiled=True)
    if paired:
        got = after(got, send, microseconds=6)
        slices = (text_up, text_down, side_up, side_down, other_up, other_down)
        room = (
            pltpu.VMEM(text_embed.shape, BF16),
            pltpu.VMEM(got.shape, BF16),
            pltpu.VMEM((4, *text_up.shape), BF16),
            pltpu.VMEM((4, *text_up.shape), BF16),
        )
        sums = jax.ShapeDtypeStruct((token_count, width), F32)
        text_normed, total = call(
            functools.partial(theirs_kernel, capacity),
            "text_theirs",
            (like(text_embed), sums),
            (other_embed, got, *slices[:4], text_gain),
            stored=tuple(range(6)),
            copies=6,
            scratch=(*room[:2], *(pltpu.VMEM((2, *text_up.shape), BF16) for _ in range(2))),
            megabytes=52,
        )
        total = call(
            theirs_more_kernel,
            "text_theirs_more",
            sums,
            (text_normed, total, *slices[4:]),
            stored=(2, 3),
            copies=2,
            scratch=tuple(pltpu.VMEM((1, *text_up.shape), BF16) for _ in range(2)),
        )
        across_down = after(across_down, text_normed)
        halves = (across_up, swap(across_up, "seq", 1), across_down, swap(across_down, "seq", 1))
        theirs = call(
            theirs_last_kernel,
            "text_theirs_last",
            like(text_embed),
            (text_normed, total, *halves),
            stored=(2, 3, 4, 5),
            copies=4,
            scratch=tuple(pltpu.VMEM((1, *text_up.shape), BF16) for _ in range(2)),
        )
        mine = call(
            functools.partial(mine_kernel, capacity),
            "text_mine",
            sums,
            (text_embed, got, *slices, *halves, text_gain),
            stored=tuple(range(12)),
            copies=12,
            scratch=room,
            megabytes=24,
        )
        return (mine + swap(theirs, "blk", 4).astype(F32)).astype(BF16)
    tokens = jnp.arange(token_count, dtype=jnp.int32).astype(BF16)
    pick = (got[:, width:][:, :1] == tokens[None, :]).astype(BF16)
    picked = lax.dot_general(pick, got[:, :width], (((0,), (0,)), ((), ())), preferred_element_type=F32)
    taken = jnp.sum(pick.astype(F32), axis=0)[:, None] > 0.5
    text_rows = jnp.where(taken, picked, text_embed.astype(F32))
    text_normed = normalize(text_rows, text_gain).astype(BF16)
    gathered_tokens = lax.all_gather(text_normed, "blk", axis=0, tiled=True)
    hidden = gelu(up_project(gathered_tokens, text_up)).astype(BF16)
    text_mlp = lax.psum_scatter(
        jnp.dot(hidden, text_down, preferred_element_type=F32).astype(BF16),
        "blk",
        scatter_dimension=0,
        tiled=True,
    ).astype(F32)
    return (text_rows + text_mlp).astype(BF16)


def solution(mesh):
    placed = (
        P(("seq", "blk"), None),
        P(),
        P("seq", None),
        P("seq"),
        P("seq", None),
        P(),
        P(),
        P(("seq", "blk"), None),
        P(("seq", "blk")),
        P(),
        P("blk", None),
        P("blk", None),
    )
    return jax.shard_map(
        per_device, mesh=mesh, in_specs=placed, out_specs=P(("seq", "blk"), None), check_vma=False
    )
```
